256 devices in a mesh: leaf: 128 (over y, x, z), rhs: 2 (over core).
Axes of the slice: x: 4, y: 4, z: 8, core: 2. Of those that a mesh axis runs over, the one named last changes fastest.
Arguments:
- values: bfloat16 [64, 1048576], P('rhs', 'leaf'), may hold values from -6 to 6
- points: float32 [3, 1048576], P(None, 'leaf'), may hold values from 0 to 1
- basis: bfloat16 [4096, 64, 256], P('leaf', 'rhs'), may hold values from -0.375 to 0.375
- near_list: int32 [4096, 9], P('leaf'), may hold values from 0 to 4095, as said below
- far_list: int32 [4096, 8], P('leaf'), may hold values from 0 to 4095, as said below
- far_count: int32 [4096], P('leaf'), may hold values from 1 to 8, as said below
- leaf_couple: bfloat16 [4096, 8, 64, 64], P('leaf'), may hold values from -0.25 to 0.25
- local_transfer: bfloat16 [2, 64, 64], replicated, may hold values from -0.75 to 0.75
- upper_transfer: bfloat16 [7, 2, 64, 64], replicated, may hold values from -0.75 to 0.75
- upper_couple: bfloat16 [7, 2, 64, 64], replicated, may hold values from -0.0234375 to 0.0234375
Outputs:
- potential: float32 [64, 1048576], P('rhs', 'leaf')
The draws below stay inside these ranges and needn't reach their ends.
Inputs may be any that keep to these rules, and one draw needn't show every extreme that they name: `near_list`: row i holds leaf indices within 4 of i; its first entry is i and its last lies exactly 4 away unless the end of the leaves cuts it. `far_list`: row i holds leaf indices within 4 of i; its last entry lies exactly 4 away unless the end of the leaves cuts it. `far_count`: some leaf uses all 8 slots.
All inputs are finite; a program needn't handle non-finite values.
Results may differ from the reference program's by a relative error of at most 0.02.
Values may be sent and summed in bfloat16 or wider, within the bound.
A program may use at most 64 MiB of HBM per device.

```python
import math
import jax
import jax.numpy as jnp
from jax import lax

LEAF = 256
K = 64
R = 64
LEAF_DEV = 32
NEAR = 9
FARL = 8
HW = 4
UPL = 7
NLEAF = 4096
NPTS = 1048576
N_LEAF = 128


def ranged_list(key, width):
    rows = jnp.arange(NLEAF, dtype=jnp.int32)
    offset = jax.random.randint(key, (NLEAF, width), -HW, HW + 1)
    sign = jax.random.randint(jax.random.fold_in(key, 1), (NLEAF,), 0, 2) * 2 - 1
    offset = offset.at[:, width - 1].set(sign * HW)
    return (offset, rows)


def draw_near_list(key, part):
    key = jax.random.fold_in(key, 11)
    offset, rows = ranged_list(key, NEAR)
    offset = offset.at[:, 0].set(0)
    return jnp.clip(rows[:, None] + offset, 0, NLEAF - 1).astype(jnp.int32)


def draw_far_list(key, part):
    key = jax.random.fold_in(key, 23)
    offset, rows = ranged_list(key, FARL)
    return jnp.clip(rows[:, None] + offset, 0, NLEAF - 1).astype(jnp.int32)


def draw_far_count(key, part):
    key = jax.random.fold_in(key, 37)
    counts = jax.random.randint(key, (NLEAF,), 1, FARL + 1)
    chosen = jax.random.randint(jax.random.fold_in(key, 1), (), 0, NLEAF)
    return counts.at[chosen].set(FARL).astype(jnp.int32)


def steps_of(key, shape, cuts, low, high):
    loudness = 1.0
    for axis_at, shards_of in cuts:
        steps = jax.random.uniform(jax.random.fold_in(jax.random.fold_in(key, 6), axis_at), (shards_of,), jnp.float32, low / len(cuts), high / len(cuts))
        loudness = loudness * jnp.repeat(jnp.exp(steps), shape[axis_at] // shards_of).reshape((-1,) + (1,) * (len(shape) - 1 - axis_at))
    return loudness


def scatter_about(stream_key, extent, spread, bound, cuts=(), kind=jnp.bfloat16):
    loudness = steps_of(stream_key, extent, cuts, -0.22, 0.18) if cuts else 1.0
    array = jax.random.normal(stream_key, extent, jnp.float32) * spread * loudness
    return jnp.minimum(jnp.maximum(array, -bound), bound).astype(kind)


def setup_inputs(seed: int = 0) -> dict:
    arg_keys = jax.random.split(jax.random.key(seed), 11)
    return {
        "values": scatter_about(arg_keys[0], (R, NPTS), 1.0, 6.0, ((0, 2), (1, 128))),
        "points": jnp.clip(1.0 * jax.random.uniform(arg_keys[1], (3, NPTS), jnp.float32) ** steps_of(arg_keys[1], (3, NPTS), ((1, 128),), -0.2, 0.2), 0.0, 1.0),
        "basis": scatter_about(arg_keys[2], (NLEAF, K, LEAF), LEAF ** -0.5, 0.375, ((0, 128), (1, 2))),
        "near_list": draw_near_list(jax.random.fold_in(arg_keys[10], 71), 0),
        "far_list": draw_far_list(jax.random.fold_in(arg_keys[10], 71), 0),
        "far_count": draw_far_count(jax.random.fold_in(arg_keys[10], 71), 0),
        "leaf_couple": scatter_about(arg_keys[6], (NLEAF, FARL, K, K), (K * FARL) ** -0.5, 0.25, ((0, 128),)),
        "local_transfer": scatter_about(arg_keys[7], (2, K, K), K ** -0.5, 0.75),
        "upper_transfer": scatter_about(arg_keys[8], (UPL, 2, K, K), K ** -0.5, 0.75),
        "upper_couple": scatter_about(arg_keys[9], (UPL, 2, K, K), (K * LEAF_DEV * N_LEAF // 4) ** -0.5, 0.0234375),
    }


WAVE = 20.0
SMOOTH = 0.05

def kernel_block(targets, sources):
    gap_x = targets[0][:, None, :, None] - sources[0][:, :, None, :]
    gap_y = targets[1][:, None, :, None] - sources[1][:, :, None, :]
    gap_z = targets[2][:, None, :, None] - sources[2][:, :, None, :]
    squared = gap_x * gap_x + gap_y * gap_y + gap_z * gap_z
    factor = 1.0 / math.sqrt(sources.shape[2] * sources.shape[3])
    return (factor * jnp.cos(WAVE * jnp.sqrt(squared)) / jnp.sqrt(squared + SMOOTH * SMOOTH)).astype(jnp.bfloat16)

def upward(level, transfer):
    pairs = level.reshape(level.shape[0] // 2, 2, level.shape[1], level.shape[2])
    return jnp.einsum('jsrk,skl->jrl', pairs.astype(jnp.float32), transfer.astype(jnp.float32)).astype(jnp.bfloat16)

def reference(values, points, basis, near_list, far_list, far_count, leaf_couple, local_transfer, upper_transfer, upper_couple):
    grouped = values.reshape(R, NLEAF, LEAF)
    spots = points.reshape(3, NLEAF, LEAF)
    leaf_coeff = jnp.einsum('ikp,rip->irk', basis.astype(jnp.float32), grouped.astype(jnp.float32)).astype(jnp.bfloat16)
    local_levels = LEAF_DEV.bit_length() - 1
    level = leaf_coeff
    for step in range(local_levels):
        level = upward(level, local_transfer)
    nodes = [level]
    for step in range(UPL - 1):
        nodes.append(upward(nodes[-1], upper_transfer[step]))
    local = None
    for step in reversed(range(UPL)):
        index = jnp.arange(nodes[step].shape[0], dtype=jnp.int32)
        side = index % 2
        sibling = nodes[step][index + 1 - 2 * side]
        term = jnp.einsum('jrk,jkl->jrl', sibling.astype(jnp.float32), upper_couple[step][side].astype(jnp.float32))
        if local is not None:
            parent = local[index // 2]
            term = term + jnp.einsum('jrl,jkl->jrk', parent.astype(jnp.float32), upper_transfer[step][side].astype(jnp.float32))
        local = term.astype(jnp.bfloat16)
    for step in range(local_levels):
        expanded = jnp.einsum('jrl,skl->jsrk', local.astype(jnp.float32), local_transfer.astype(jnp.float32))
        expanded = expanded.reshape(-1, R, K)
        if step < local_levels - 1:
            local = expanded.astype(jnp.bfloat16)
    leaf_down = expanded
    block = 16

    def one_block(start):
        targets = lax.dynamic_slice_in_dim(spots, start, block, 1)
        near_index = lax.dynamic_slice_in_dim(near_list, start, block, 0)
        sources = spots[:, near_index]
        source_values = grouped[:, near_index]
        kernel = kernel_block(targets, sources)
        near = jnp.einsum('gnpq,rgnq->rgp', kernel.astype(jnp.float32), source_values.astype(jnp.float32))
        far_index = lax.dynamic_slice_in_dim(far_list, start, block, 0)
        counts = lax.dynamic_slice_in_dim(far_count, start, block, 0)
        live = jnp.arange(FARL, dtype=jnp.int32)[None, :] < counts[:, None]
        picked = jnp.where(live[:, :, None, None], leaf_coeff[far_index].astype(jnp.float32), 0.0)
        couple = lax.dynamic_slice_in_dim(leaf_couple, start, block, 0).astype(jnp.float32)
        far = jnp.einsum('gsrk,gskl->grl', picked, couple) + lax.dynamic_slice_in_dim(leaf_down, start, block, 0)
        leaf_local = far.astype(jnp.bfloat16)
        bases = lax.dynamic_slice_in_dim(basis, start, block, 0).astype(jnp.float32)
        return near + jnp.einsum('gkp,grk->rgp', bases, leaf_local.astype(jnp.float32))
    starts = jnp.arange(NLEAF // block, dtype=jnp.int32) * block
    blocks = lax.map(one_block, starts)
    return jnp.transpose(blocks, (1, 0, 2, 3)).reshape(R, NPTS)
```

```python
import functools
import math

import jax
import jax.numpy as jnp
import numpy as np
from jax import lax
from jax.experimental import pallas as pl
from jax.experimental.pallas import tpu as pltpu
from jax.sharding import PartitionSpec as P

MESH = pl.DeviceIdType.MESH
F32 = jnp.float32
BF16 = jnp.bfloat16
HW = 4
WAVE = 20.0
SMOOTH = 0.05
LEAF = 256
OWN = 16
EXT = OWN + 2 * HW
SCALE = WAVE / (2 * math.pi)
SOFT = SCALE * SCALE * SMOOTH * SMOOTH
DEGREE = 5


def cosine_fit():
    nodes = 0.125 + 0.125 * np.cos(np.pi * (np.arange(64) + 0.5) / 64)
    series = np.polynomial.chebyshev.Chebyshev.fit(
        nodes, np.cos(2 * np.pi * np.sqrt(nodes)), DEGREE, domain=[0, 0.25]
    )
    power = series.convert(kind=np.polynomial.Polynomial).coef
    return [float(v) for v in power * SCALE / math.sqrt(9 * LEAF)]


COSINE = cosine_fit()


def entries(scaled):
    scaled = jnp.maximum(scaled, 1e-12)
    turns = scaled * lax.rsqrt(scaled)
    rest = turns - jnp.round(turns)
    square = rest * rest
    poly = COSINE[DEGREE]
    for power in range(DEGREE - 1, -1, -1):
        poly = poly * square + COSINE[power]
    return (poly * lax.rsqrt(scaled + SOFT)).astype(BF16)


def dot(a, b, left=1, right=0):
    return lax.dot_general(a, b, (((left,), (right,)), ((), ())), preferred_element_type=F32)


def cols(leaf, count=1):
    return pl.ds(pl.multiple_of(leaf * LEAF, LEAF), count * LEAF)


def diagonal(block):
    block = block.astype(F32)
    zero = jnp.zeros_like(block)
    top = jnp.concatenate([block, zero], axis=1)
    low = jnp.concatenate([zero, block], axis=1)
    return jnp.concatenate([top, low], axis=0).astype(BF16)


def kernel(
    n,
    zn,
    values,
    points,
    basis,
    near_list,
    far_list,
    far_count,
    couple,
    local_transfer,
    upper_transfer,
    upper_couple,
    out,
    vx,
    px,
    fa,
    fb,
    bx,
    cv,
    acc,
    dco,
    lev,
    ldown,
    nodes,
    pair,
    zb,
    gb,
    wup,
    wdn,
    wld,
    wleaf,
    count,
    loc,
    ssem,
    rsem,
    zs,
    zr,
    gs,
    gr,
    osem,
):
    d = lax.axis_index("leaf")
    c = lax.axis_index("rhs")
    p = 1 - c
    gn = n // zn
    z = lax.rem(d, zn)
    g = d // zn
    after = lax.rem(d + 1, n)
    before = lax.rem(d + n - 1, n)
    upl = (n - 1).bit_length()
    zl = (zn - 1).bit_length()

    barrier = pltpu.get_barrier_semaphore()

    def greet(leaf, core):
        pl.semaphore_signal(barrier, inc=1, device_id=(leaf, core), device_id_type=MESH)

    side_dev = lax.rem(d + n - 1 + 2 * c, n)
    greet(d, p)
    greet(side_dev, 0)
    greet(side_dev, 1)

    @pl.loop(1, zn)
    def _(t):
        greet(g * zn + lax.rem(z + t, zn), c)

    @pl.loop(1, gn)
    def _(t):
        greet(lax.rem(g + t, gn) * zn + z, c)

    def local(src, dst, k):
        copy = pltpu.make_async_copy(src, dst, loc.at[k])
        copy.start()
        return copy

    lp = local(points.at[:, cols(12 * c, 20)], px.at[:, cols(4 - 4 * c, 20)], 0)
    lv = local(
        values.at[:, cols(12 * c, 20)], vx.at[pl.ds(32 * c, 32), cols(4 - 4 * c, 20)], 1
    )
    lb = local(basis.at[pl.ds(16 * c, 16)], bx.at[:, pl.ds(32 * c, 32), :], 2)
    lc = local(couple.at[pl.ds(16 * c, 16)], cv, 3)

    pl.semaphore_wait(barrier, 3 + (zn - 1) + (gn - 1))

    def send(src, dst, k, r, leaf, core):
        copy = pltpu.make_async_remote_copy(
            src_ref=src,
            dst_ref=dst,
            send_sem=ssem.at[k],
            recv_sem=rsem.at[r],
            device_id=(leaf, core),
            device_id_type=MESH,
        )
        copy.start()
        return copy

    own = pl.ds(32 * c, 32)
    sv = send(values.at[:, cols(12 * p, 20)], vx.at[own, cols(4 - 4 * p, 20)], 0, 0, d, p)
    sb = send(basis.at[pl.ds(16 * p, 16)], bx.at[:, own, :], 1, 1, d, p)
    sp = send(
        points.at[:, cols(28 * p, 4)],
        px.at[:, cols(20 * c, 4)],
        2,
        2,
        lax.rem(d + n + 1 - 2 * c, n),
        c,
    )
    sr0 = send(values.at[:, cols(28, 4)], vx.at[own, cols(0, 4)], 3, 3 + c, after, 0)
    sr1 = send(values.at[:, cols(0, 4)], vx.at[own, cols(20, 4)], 4, 3 + c, before, 1)

    for s in range(2):
        t = local_transfer[s]
        wup[0, pl.ds(128 * s, 128), :] = diagonal(t)
        td = t.astype(F32).T
        wld[s] = diagonal(td)
        zero = jnp.zeros((64, 64), F32)
        wide = jnp.concatenate([td, zero], axis=1).astype(BF16)
        none = jnp.zeros((64, 128), BF16)
        wleaf[0, pl.ds(0, 64), pl.ds(128 * s, 128)] = wide
        wleaf[0, pl.ds(64, 64), pl.ds(128 * s, 128)] = none
        wleaf[1, pl.ds(0, 64), pl.ds(128 * s, 128)] = none
        wleaf[1, pl.ds(64, 64), pl.ds(128 * s, 128)] = wide

    @pl.loop(0, upl)
    def _(u):
        for s in range(2):
            t = upper_transfer[u, s]
            wup[u + 1, pl.ds(128 * s, 128), :] = diagonal(t)
            wdn[2 * u + s, pl.ds(0, 128), :] = diagonal(upper_couple[u, s])
            wdn[2 * u + s, pl.ds(128, 128), :] = diagonal(t.astype(F32).T)

    @pl.loop(0, OWN)
    def _(i):
        row = 16 * c + i
        slots = [near_list[s, row] - (d * 32 + row) for s in range(9)]
        for o in range(9):
            total = jnp.float32(0)
            for s in range(9):
                total = total + jnp.where(slots[s] == o - HW, jnp.float32(1), jnp.float32(0))
            count[i * 9 + o] = total

    @pl.loop(0, HW * 9)
    def _(i):
        count[OWN * 9 + i] = jnp.float32(0)

    acc[...] = jnp.zeros_like(acc)
    dco[EXT] = jnp.zeros((64, 128), BF16)

    rows = lax.broadcasted_iota(jnp.int32, (8, LEAF), 0)

    def factors(e):
        at = cols(e)
        x = (px[:, at] - 0.5) * SCALE
        x = jnp.concatenate([x, jnp.zeros((5, LEAF), F32)], axis=0)
        high = x.astype(BF16).astype(F32)
        low = (x - high).astype(BF16).astype(F32)
        both = high + low
        norm = jnp.sum(both * both, axis=0, keepdims=True)
        n1 = norm.astype(BF16).astype(F32)
        n2 = (norm - n1).astype(BF16).astype(F32)
        n3 = (norm - n1 - n2).astype(BF16).astype(F32)
        norms = jnp.where(
            rows == 3, n1, jnp.where(rows == 4, n2, jnp.where(rows == 5, n3, 0.0))
        )
        ones = jnp.where((rows >= 3) & (rows <= 5), 1.0, 0.0)
        fa[:, at] = jnp.concatenate([high + norms, high + ones, low, low], axis=0).astype(BF16)
        fb[:, at] = jnp.concatenate(
            [ones - 2 * high, norms - 2 * low, -2 * high, -2 * low], axis=0
        ).astype(BF16)

    lp.wait()

    @pl.loop(0, 20)
    def _(e):
        factors(e + 4 - 4 * c)

    def near_main(i):
        e = i + HW
        left = fa[:, cols(e)]
        mine = vx[:, cols(e)]
        total = None
        parts = []
        for o in range(HW + 1):
            block = entries(dot(left, fb[:, cols(e + o)], 0, 0))
            term = dot(vx[:, cols(e + o)], block, 1, 1) * count[i * 9 + HW + o]
            total = term if total is None else total + term
            if o:
                parts.append(dot(mine, block, 1, 0) * count[(i + o) * 9 + HW - o])
        acc[:, cols(e, HW + 1)] += jnp.concatenate([total] + parts, axis=1)

    def near_rim(w):
        for b in range(HW + 1):
            first = b < HW - w
            e = jnp.where(first, w + b, b - 1)
            j = jnp.where(first, w, 3 - w)
            block = entries(dot(fa[:, cols(e)], fb[:, cols(j + HW)], 0, 0))
            acc[:, cols(j + HW)] += dot(vx[:, cols(e)], block, 1, 0) * count[j * 9 + e - j]

    def batch(start):
        @pl.loop(start, start + 4, step=2)
        def _(i):
            near_main(i)
            near_main(i + 1)

    lv.wait()
    sv.wait_recv()
    lb.wait()
    sb.wait_recv()
    lanes = lax.broadcasted_iota(jnp.int32, (32, 128), 1) < 64

    @pl.loop(0, OWN, step=4)
    def _(i0):
        for k in range(4):
            i = i0 + k
            twice = jnp.concatenate([bx[i], bx[i]], axis=0)
            full = dot(vx[:, cols(i + HW)], twice, 1, 1)
            dco[i + HW] = full.astype(BF16)
            lev[i] = jnp.where(lanes, full[0:32], full[32:64]).astype(BF16)

    sc0 = send(
        dco.at[pl.ds(4, 4)], dco.at[pl.ds(20, 4)], 5, 5, lax.rem(d + n - p, n), p
    )
    sc1 = send(dco.at[pl.ds(16, 4)], dco.at[pl.ds(0, 4)], 6, 6, lax.rem(d + c, n), p)

    def joined(read, m):
        return jnp.concatenate(
            [
                jnp.concatenate([read(2 * j), read(2 * j + 1)], axis=1)
                for j in range(m)
            ],
            axis=0,
        )

    def upward(src, at, dst, to, m, weight):
        whole = dot(joined(lambda j: src[at + j], m), wup[weight]).astype(BF16)
        for j in range(m):
            dst[to + j] = whole[32 * j : 32 * j + 32]

    upward(lev, 0, lev, 16, 8, 0)
    upward(lev, 16, lev, 24, 4, 0)
    upward(lev, 24, lev, 28, 2, 0)
    whole = dot(joined(lambda j: lev[28 + j], 1), wup[0]).astype(BF16)
    lev[30] = whole
    pair[c] = whole
    sn = send(lev.at[30], pair.at[c], 7, 7, d, p)

    batch(0)

    sn.wait_recv()
    root = dot(joined(lambda j: pair[j], 1), wup[0]).astype(BF16)
    zb[z] = root

    def ring(buf, slot, sems, recvs, t, leaf):
        return pltpu.make_async_remote_copy(
            src_ref=buf.at[slot],
            dst_ref=buf.at[slot],
            send_sem=sems.at[t],
            recv_sem=recvs.at[t],
            device_id=(leaf, c),
            device_id_type=MESH,
        )

    def z_copy(t):
        return ring(zb, z, zs, zr, t - 1, g * zn + lax.rem(z + t, zn))

    def g_copy(t):
        return ring(gb, g, gs, gr, t - 1, lax.rem(g + t, gn) * zn + z)

    @pl.loop(1, zn)
    def _(t):
        z_copy(t).start()

    batch(4)

    @pl.loop(1, zn)
    def _(t):
        z_copy(t).wait_recv()

    at = 0
    m = zn
    weight = 1
    while m > 2:
        upward(zb, at, zb, at + m, m // 2, weight)
        at, m, weight = at + m, m // 2, weight + 1
    gb[g] = dot(joined(lambda j: zb[at + j], 1), wup[weight]).astype(BF16)
    weight += 1

    @pl.loop(1, gn)
    def _(t):
        g_copy(t).start()

    batch(8)

    sp.wait_recv()

    @pl.loop(0, 4)
    def _(e):
        factors(e + 20 * c)

    for r in range(2):
        pltpu.make_async_copy(
            vx.at[pl.ds(0, 32), cols(0, 4)], vx.at[pl.ds(0, 32), cols(0, 4)], rsem.at[3 + r]
        ).wait()

    batch(12)

    @pl.loop(0, 2)
    def _(w):
        near_rim(w)

    @pl.loop(1, gn)
    def _(t):
        g_copy(t).wait_recv()

    at = 0
    m = gn
    while m > 2:
        upward(gb, at, gb, at + m, m // 2, weight)
        at, m, weight = at + m, m // 2, weight + 1

    down = jnp.zeros((32, 128), BF16)
    for u in range(upl - 1, -1, -1):
        if u >= zl:
            buf, size, index, step = gb, gn, g, u - zl
        else:
            buf, size, index, step = zb, zn, z, u
        base = 2 * size - 2 * (size >> step)
        here = index // 2**step
        side = lax.rem(here, 2)
        sibling = buf[base + here + 1 - 2 * side]
        both = jnp.concatenate([sibling, down], axis=1)
        down = dot(both, wdn[2 * u + side]).astype(BF16)
    nodes[0] = dot(down, wld[c]).astype(BF16)
    at, m = 0, 1
    while m < 8:
        whole = jnp.concatenate([nodes[at + j] for j in range(m)], axis=0)
        for s in range(2):
            child = dot(whole, wld[s]).astype(BF16)
            for j in range(m):
                nodes[at + m + 2 * j + s] = child[32 * j : 32 * j + 32]
        at, m = at + m, 2 * m
    whole = jnp.concatenate([nodes[at + j] for j in range(8)], axis=0)
    for h in range(2):
        low = dot(whole, wleaf[h])
        for j in range(8):
            for s in range(2):
                ldown[2 * j + s, pl.ds(32 * h, 32), :] = low[
                    32 * j : 32 * j + 32, 128 * s : 128 * s + 128
                ]

    sc0.wait_recv()
    sc1.wait_recv()
    lc.wait()
    wide = lax.broadcasted_iota(jnp.int32, (64, 128), 1) < 64
    pick0 = jnp.where(wide, 1.0, 0.0).astype(BF16)
    pick1 = jnp.where(wide, 0.0, 1.0).astype(BF16)

    def result(i):
        row = 16 * c + i
        first = d * 32 + 16 * c - HW
        used = far_count[row]
        at = [jnp.where(s < used, far_list[s, row] - first, EXT) for s in range(8)]
        coeffs = jnp.concatenate(
            [dco[at[2 * q]] * pick0 + dco[at[2 * q + 1]] * pick1 for q in range(4)], axis=1
        )
        far = dot(coeffs, cv[i].reshape(512, 64)) + ldown[i][:, 0:64]
        acc[:, cols(i + HW)] += dot(far.astype(BF16), bx[i])

    def out_local(k):
        return pltpu.make_async_copy(
            acc.at[own, cols(HW + 4 * k, 4)], out.at[:, cols(16 * c + 4 * k, 4)], loc.at[4 + k]
        )

    def out_send(k):
        return pltpu.make_async_remote_copy(
            src_ref=acc.at[pl.ds(32 * p, 32), cols(HW + 4 * k, 4)],
            dst_ref=out.at[:, cols(16 * c + 4 * k, 4)],
            send_sem=osem.at[k],
            recv_sem=osem.at[4 + k],
            device_id=(d, p),
            device_id_type=MESH,
        )

    @pl.loop(0, 4)
    def _(k):
        for i in range(4):
            result(4 * k + i)
        out_send(k).start()
        out_local(k).start()

    for copy in (sv, sb, sp, sr0, sr1, sc0, sc1, sn):
        copy.wait_send()

    @pl.loop(1, zn)
    def _(t):
        z_copy(t).wait_send()

    @pl.loop(1, gn)
    def _(t):
        g_copy(t).wait_send()

    @pl.loop(0, 4)
    def _(k):
        out_local(k).wait()
        out_send(k).wait()


def solution(mesh):
    n = mesh.shape["leaf"]
    zn = 8 if n >= 64 else 2
    gn = n // zn
    upl = (n - 1).bit_length()
    hbm = pl.BlockSpec(memory_space=pl.ANY)
    vmem = pl.BlockSpec(memory_space=pltpu.VMEM)
    smem = pl.BlockSpec(memory_space=pltpu.SMEM)
    dma = pltpu.SemaphoreType.DMA

    def on_device(values, points, basis, near_list, far_list, *rest):
        return pl.pallas_call(
            functools.partial(kernel, n, zn),
            out_shape=jax.ShapeDtypeStruct((32, 8192), F32),
            in_specs=[hbm, hbm, hbm, smem, smem, smem, hbm, vmem, vmem, vmem],
            out_specs=hbm,
            scratch_shapes=[
                pltpu.VMEM((64, EXT * LEAF), BF16),
                pltpu.VMEM((3, EXT * LEAF), F32),
                pltpu.VMEM((32, EXT * LEAF), BF16),
                pltpu.VMEM((32, EXT * LEAF), BF16),
                pltpu.VMEM((OWN, 64, LEAF), BF16),
                pltpu.VMEM((OWN, 8, 64, 64), BF16),
                pltpu.VMEM((64, EXT * LEAF), F32),
                pltpu.VMEM((EXT + 1, 64, 128), BF16),
                pltpu.VMEM((32, 32, 128), BF16),
                pltpu.VMEM((OWN, 64, 128), F32),
                pltpu.VMEM((16, 32, 128), BF16),
                pltpu.VMEM((2, 32, 128), BF16),
                pltpu.VMEM((2 * zn, 32, 128), BF16),
                pltpu.VMEM((2 * gn, 32, 128), BF16),
                pltpu.VMEM((upl + 1, 256, 128), BF16),
                pltpu.VMEM((2 * upl, 256, 128), BF16),
                pltpu.VMEM((2, 128, 128), BF16),
                pltpu.VMEM((2, 128, 256), BF16),
                pltpu.SMEM(((OWN + HW) * 9,), F32),
                dma((8,)),
                dma((8,)),
                dma((8,)),
                dma((zn - 1,)),
                dma((zn - 1,)),
                dma((gn - 1,)),
                dma((gn - 1,)),
                dma((8,)),
            ],
            compiler_params=pltpu.CompilerParams(
                collective_id=0, has_side_effects=True, vmem_limit_bytes=60 * 2**20
            ),
            name="h2_matvec",
        )(values, points, basis, near_list.T, far_list.T, *rest)

    placed = (
        P("rhs", "leaf"),
        P(None, "leaf"),
        P("leaf", "rhs", None),
        P("leaf", None),
        P("leaf", None),
        P("leaf"),
        P("leaf", None, None, None),
        P(),
        P(),
        P(),
    )
    return jax.shard_map(
        on_device, mesh=mesh, in_specs=placed, out_specs=P("rhs", "leaf"), check_vma=False
    )
```

```python
import functools
import math

import jax
import jax.numpy as jnp
import numpy as np
from jax import lax
from jax.experimental import pallas as pl
from jax.experimental.pallas import tpu as pltpu
from jax.sharding import PartitionSpec as P

MESH = pl.DeviceIdType.MESH
F32 = jnp.float32
BF16 = jnp.bfloat16
HW = 4
WAVE = 20.0
SMOOTH = 0.05
LEAF = 256
OWN = 16
EXT = OWN + 2 * HW
SCALE = WAVE / (2 * math.pi)
SOFT = SCALE * SCALE * SMOOTH * SMOOTH
DEGREE = 4
SCHEDULE = (
    (5, 5, 8, 10, 14, 5),
    (4, 5, 7, 10, 13, 4),
    (4, 4, 6, 9, 12, 4),
    (3, 3, 5, 8, 10, 3),
    (2, 2, 4, 7, 9, 2),
)


def cosine_fit():
    nodes = 0.125 + 0.125 * np.cos(np.pi * (np.arange(64) + 0.5) / 64)
    series = np.polynomial.chebyshev.Chebyshev.fit(
        nodes, np.cos(2 * np.pi * np.sqrt(nodes)), DEGREE, domain=[0, 0.25]
    )
    power = series.convert(kind=np.polynomial.Polynomial).coef
    return [float(v) for v in power * SCALE / math.sqrt(9 * LEAF)]


COSINE = cosine_fit()


def entries(scaled):
    scaled = jnp.maximum(scaled, 1e-12)
    turns = scaled * lax.rsqrt(scaled)
    rest = turns - jnp.round(turns)
    square = rest * rest
    poly = COSINE[DEGREE]
    for power in range(DEGREE - 1, -1, -1):
        poly = poly * square + COSINE[power]
    return (poly * lax.rsqrt(scaled + SOFT)).astype(BF16)


def dot(a, b, left=1, right=0):
    return lax.dot_general(a, b, (((left,), (right,)), ((), ())), preferred_element_type=F32)


def cols(leaf, count=1):
    return pl.ds(pl.multiple_of(leaf * LEAF, LEAF), count * LEAF)


def diagonal(block):
    block = block.astype(F32)
    zero = jnp.zeros_like(block)
    top = jnp.concatenate([block, zero], axis=1)
    low = jnp.concatenate([zero, block], axis=1)
    return jnp.concatenate([top, low], axis=0).astype(BF16)


def kernel(
    dims,
    values,
    points,
    basis,
    near_list,
    far_list,
    far_count,
    couple,
    local_transfer,
    upper_transfer,
    upper_couple,
    out,
    vx,
    px,
    fa,
    fb,
    bx,
    cv,
    kb,
    acc,
    dco,
    fco,
    lev,
    ldown,
    yfar,
    nodes,
    pair,
    zb,
    xb,
    yb,
    wup,
    wdn,
    wld,
    wsel,
    wleaf,
    tally,
    tally_next,
    count,
    count_next,
    spill,
    loc,
    ssem,
    rsem,
    zs,
    zr,
    xs,
    xr,
    ys,
    yr,
):
    yn, xn, zn = dims
    n = yn * xn * zn
    d = lax.axis_index("leaf")
    c = lax.axis_index("rhs")
    p = 1 - c
    z = lax.rem(d, zn)
    x = lax.rem(d // zn, xn)
    y = d // (zn * xn)
    after = lax.rem(d + 1, n)
    before = lax.rem(d + n - 1, n)
    beside = lax.rem(d + n - 1 + 2 * c, n)
    upl = (n - 1).bit_length()
    own = pl.ds(32 * c, 32)

    barrier = pltpu.get_barrier_semaphore()

    def greet(leaf, core):
        pl.semaphore_signal(barrier, inc=1, device_id=(leaf, core), device_id_type=MESH)

    def z_peer(t):
        return d - z + lax.rem(z + t, zn)

    def x_peer(t):
        return d + (lax.rem(x + t, xn) - x) * zn

    def y_peer(t):
        return d + (lax.rem(y + t, yn) - y) * zn * xn

    stages = (
        (zb, zn, z, zs, zr, z_peer),
        (xb, xn, x, xs, xr, x_peer),
        (yb, yn, y, ys, yr, y_peer),
    )

    greet(d, p)
    greet(before, 1)
    greet(after, 0)

    @pl.when(c == 1)
    def _():
        greet(after, 1)

    for _, size, _, _, _, peer in stages:

        @pl.loop(1, size)
        def _(t):
            greet(peer(t), c)

    def local(src, dst, k):
        return pltpu.make_async_copy(src, dst, loc.at[k])

    lp = local(points.at[:, cols(12 * c, 20)], px.at[:, cols(4 - 4 * c, 20)], 0)
    lv = local(
        values.at[:, cols(12 * c, 20)], vx.at[own, cols(4 - 4 * c, 20)], 1
    )
    lb = local(basis, bx.at[:, own, :], 2)
    lc = local(couple, cv, 3)
    lf = local(dco.at[:, own, :], fco.at[pl.ds(16 * c + HW, OWN)], 4)
    lt = local(tally, count, 6)
    lu = local(tally_next, count_next, 7)
    ln = local(acc.at[own, cols(HW, OWN)], out.at[:, cols(16 * c, OWN)], 5)
    for copy in (lp, lv, lb, lc):
        copy.start()

    def remote(src, dst, k, r, leaf, core):
        return pltpu.make_async_remote_copy(
            src_ref=src,
            dst_ref=dst,
            send_sem=ssem.at[k],
            recv_sem=rsem.at[r],
            device_id=(leaf, core),
            device_id_type=MESH,
        )

    sv = remote(values.at[:, cols(12 * p, 20)], vx.at[own, cols(4 - 4 * p, 20)], 0, 0, d, p)
    sb = remote(
        basis.at[pl.ds(16 * p, 16)], bx.at[pl.ds(16 * p, 16), own, :], 1, 1, d, p
    )
    sl = remote(
        basis.at[pl.ds(16 * c, 16)], bx.at[pl.ds(16 * c, 16), own, :], 2, 2, d, p
    )
    sp = remote(points.at[:, cols(0, 4)], px.at[:, cols(20, 4)], 3, 3, before, 1)
    st = remote(tally, tally_next, 4, 11, before, 1)
    sr = remote(values.at[:, cols(0, 4)], vx.at[own, cols(20, 4)], 5, 4 + c, before, 1)
    ss = remote(
        acc.at[:, cols(20, 4)], spill, 11, 12, lax.rem(d + c, n), p
    )
    sc = remote(
        dco.at[:, pl.ds(32 * p, 32), :], fco.at[pl.ds(16 * c + HW, OWN)], 6, 6, d, p
    )
    se0, se1 = [
        remote(
            dco.at[pl.ds(12 * c, HW), pl.ds(32 * q, 32), :],
            fco.at[pl.ds(36 * p, HW)],
            7 + q,
            7 + c,
            beside,
            q,
        )
        for q in range(2)
    ]
    sn = remote(lev.at[30], pair.at[c], 9, 9, d, p)
    so = remote(
        acc.at[pl.ds(32 * p, 32), cols(HW, OWN)], out.at[:, cols(16 * c, OWN)], 10, 10, d, p
    )

    def arrived(ref, r):
        pltpu.make_async_copy(ref, ref, rsem.at[r]).wait()

    def ring(stage, t):
        buf, size, me, sems, recvs, peer = stage
        return pltpu.make_async_remote_copy(
            src_ref=buf.at[me],
            dst_ref=buf.at[me],
            send_sem=sems.at[t - 1],
            recv_sem=recvs.at[t - 1],
            device_id=(peer(t), c),
            device_id_type=MESH,
        )

    def ring_start(stage):
        @pl.loop(1, stage[1])
        def _(t):
            ring(stage, t).start()

    def ring_recv(stage):
        @pl.loop(1, stage[1])
        def _(t):
            ring(stage, t).wait_recv()

    def weights():
        zero = jnp.zeros((64, 64), F32)
        none = jnp.zeros((64, 128), BF16)
        for s in range(2):
            t = local_transfer[s]
            wup[0, pl.ds(128 * s, 128), :] = diagonal(t)
            td = t.astype(F32).T
            wld[:, pl.ds(128 * s, 128)] = diagonal(td)
            wsel[pl.ds(64 * c, 64), pl.ds(128 * s, 128)] = jnp.concatenate(
                [td, td], axis=1
            ).astype(BF16)
            wsel[pl.ds(64 * p, 64), pl.ds(128 * s, 128)] = none
            wide = jnp.concatenate([td, zero], axis=1).astype(BF16)
            wleaf[0, pl.ds(0, 64), pl.ds(128 * s, 128)] = wide
            wleaf[0, pl.ds(64, 64), pl.ds(128 * s, 128)] = none
            wleaf[1, pl.ds(0, 64), pl.ds(128 * s, 128)] = none
            wleaf[1, pl.ds(64, 64), pl.ds(128 * s, 128)] = wide
        for u in range(upl):
            for s in range(2):
                t = upper_transfer[u, s]
                if u < upl - 1:
                    wup[u + 1, pl.ds(128 * s, 128), :] = diagonal(t)
                wdn[2 * u + s, pl.ds(0, 128), :] = diagonal(upper_couple[u, s])
                wdn[2 * u + s, pl.ds(128, 128), :] = diagonal(t.astype(F32).T)

    def counts():
        leaf = lax.broadcasted_iota(jnp.int32, (9, 32), 1)
        offset = near_list[...] - leaf - d * 32
        tally[...] = jnp.zeros_like(tally)
        for o in range(9):
            same = jnp.where(offset == o - HW, 1.0, 0.0)
            tally[pl.ds(o, 1), pl.ds(0, 32)] = jnp.sum(same, axis=0, keepdims=True)
        lt.start()

    def often(i, o):
        row = 16 * c + i
        return jnp.where(
            row < 32, count[o, row], count_next[o, jnp.maximum(row - 32, 0)]
        )

    rows = lax.broadcasted_iota(jnp.int32, (8, LEAF), 0)

    def factors(e):
        at = cols(e)
        pts = (px[:, at] - 0.5) * SCALE
        pts = jnp.concatenate([pts, jnp.zeros((5, LEAF), F32)], axis=0)
        high = pts.astype(BF16).astype(F32)
        low = (pts - high).astype(BF16).astype(F32)
        both = high + low
        norm = jnp.sum(both * both, axis=0, keepdims=True)
        n1 = norm.astype(BF16).astype(F32)
        n2 = (norm - n1).astype(BF16).astype(F32)
        n3 = (norm - n1 - n2).astype(BF16).astype(F32)
        norms = jnp.where(
            rows == 3, n1, jnp.where(rows == 4, n2, jnp.where(rows == 5, n3, 0.0))
        )
        ones = jnp.where((rows >= 3) & (rows <= 5), 1.0, 0.0)
        fa[:, at] = jnp.concatenate([high + norms, high + ones, low, low], axis=0).astype(BF16)
        fb[:, at] = jnp.concatenate(
            [ones - 2 * high, norms - 2 * low, -2 * high, -2 * low], axis=0
        ).astype(BF16)

    def kernel_unit(u):
        for h in range(2):
            q = 2 * u + h
            for b in range(HW + 1):
                kb[q, :, pl.ds(b * LEAF, LEAF)] = entries(
                    dot(fa[:, cols(q + HW)], fb[:, cols(q + HW + b)], 0, 0)
                )

    def near_main(i):
        e = i + HW
        mine = vx[:, cols(e)]
        total = None
        parts = []
        for o in range(HW + 1):
            block = kb[i, :, pl.ds(o * LEAF, LEAF)]
            term = dot(vx[:, cols(e + o)], block, 1, 1) * often(i, HW + o)
            total = term if total is None else total + term
            if o:
                parts.append(dot(mine, block, 1, 0) * often(i + o, HW - o))
        acc[:, cols(e, HW + 1)] += jnp.concatenate([total] + parts, axis=1)

    def joined(read, m):
        return jnp.concatenate(
            [jnp.concatenate([read(2 * j), read(2 * j + 1)], axis=1) for j in range(m)], axis=0
        )

    def upward(src, at, dst, to, m, weight):
        whole = dot(joined(lambda j: src[at + j], m), wup[weight]).astype(BF16)
        for j in range(m):
            dst[to + j] = whole[32 * j : 32 * j + 32]

    def levels(stage, weight):
        buf, size = stage[:2]
        at, m = 0, size
        while m > 2:
            upward(buf, at, buf, at + m, m // 2, weight)
            at, m, weight = at + m, m // 2, weight + 1
        return at, weight

    def merged(stage, weight):
        at, weight = levels(stage, weight)
        return dot(joined(lambda j: stage[0][at + j], 1), wup[weight]).astype(BF16)

    def depth(size):
        return (size - 1).bit_length()

    def enter():
        pl.semaphore_wait(barrier, 3 + c + (zn - 1) + (xn - 1) + (yn - 1))
        for copy in (sb, sv):
            copy.start()

        @pl.when(c == 0)
        def _():
            sp.start()
            st.start()

        sr.start()
        sl.start()
        weights()

    lanes = lax.broadcasted_iota(jnp.int32, (32, 128), 1) < 64

    def coefficients():
        lv.wait()
        sv.wait_recv()
        lb.wait()
        sb.wait_recv()
        lt.wait()

        @pl.loop(0, OWN, step=8)
        def _(i0):
            for k in range(8):
                i = i0 + k
                mine = bx[16 * c + i]
                full = dot(
                    vx[:, cols(i + HW)], jnp.concatenate([mine, mine], axis=0), 1, 1
                )
                dco[i] = full.astype(BF16)
                lev[i] = jnp.where(lanes, full[0:32], full[32:64]).astype(BF16)

        upward(lev, 0, lev, 16, 8, 0)
        upward(lev, 16, lev, 24, 4, 0)
        upward(lev, 24, lev, 28, 2, 0)
        whole = dot(joined(lambda j: lev[28 + j], 1), wup[0]).astype(BF16)
        lev[30] = whole
        pair[c] = whole
        sn.start()
        for copy in (sc, se0, se1, lf):
            copy.start()

    def z_stage():
        sn.wait_recv()
        zb[z] = dot(joined(lambda j: pair[j], 1), wup[0]).astype(BF16)
        ring_start(stages[0])

    def x_stage():
        ring_recv(stages[0])
        xb[x] = merged(stages[0], 1)
        ring_start(stages[1])

    def y_stage():
        ring_recv(stages[1])
        yb[y] = merged(stages[1], 1 + depth(zn))
        ring_start(stages[2])

    def rims():
        @pl.when(c == 1)
        def _():
            sp.wait_recv()
            for r in range(2):
                arrived(vx.at[pl.ds(0, 32), cols(20, 4)], 4 + r)
            st.wait_recv()
            lu.start()
            for e in range(4):
                factors(e + 20)
            lu.wait()

    def place(k):
        at = SCHEDULE[-1][k]
        for row in range(len(SCHEDULE) - 1):
            at = jnp.where(z == row, SCHEDULE[row][k], at)
        return at

    last = place(5)
    events = tuple(
        (place(k), event)
        for k, event in enumerate((enter, coefficients, z_stage, x_stage, y_stage))
    ) + ((last, rims), (last + 4, ss.start))

    lp.wait()

    @pl.loop(0, 20, step=4)
    def _(e):
        for k in range(4):
            factors(e + k + 4 - 4 * c)

    acc[...] = jnp.zeros_like(acc)
    fco[40] = jnp.zeros((32, 128), BF16)
    counts()

    @pl.loop(0, 16)
    def _(t):
        for when, event in events:
            pl.when(t == when)(event)

        kernels = (t < last + 2) | ((t >= last + 4) & (t < 10))

        @pl.when(kernels)
        def _():
            kernel_unit(jnp.where(t < last, t, jnp.where(t < last + 2, t - last + 6, t - 4)))

        @pl.when(jnp.logical_not(kernels))
        def _():
            i = 2 * jnp.where(t < last + 4, t - last + 4, t - 10)
            near_main(i)
            near_main(i + 1)

    ss.wait_recv()
    acc[:, cols(HW, HW)] += spill[...]
    so.start()
    ln.start()

    lf.wait()
    sc.wait_recv()
    for r in range(2):
        arrived(fco.at[pl.ds(0, HW)], 7 + r)
    lc.wait()
    pick0 = jnp.where(lanes, 1.0, 0.0).astype(BF16)
    pick1 = jnp.where(lanes, 0.0, 1.0).astype(BF16)

    @pl.loop(0, 32, step=4)
    def _(i0):
        for k in range(4):
            i = i0 + k
            used = far_count[i]
            at = [jnp.where(s < used, far_list[s, i] - d * 32 + HW, 40) for s in range(8)]
            coeffs = jnp.concatenate(
                [fco[at[2 * q]] * pick0 + fco[at[2 * q + 1]] * pick1 for q in range(4)], axis=1
            )
            yfar[i] = dot(coeffs, cv[i].reshape(512, 64))

    ring_recv(stages[2])
    levels(stages[2], 1 + depth(zn) + depth(xn))

    down = jnp.zeros((32, 128), BF16)
    u = upl - 1
    for buf, size, me, _, _, _ in reversed(stages):
        for step in range(depth(size) - 1, -1, -1):
            here = me // 2**step
            side = lax.rem(here, 2)
            sibling = buf[2 * size - 2 * (size >> step) + here + 1 - 2 * side]
            both = jnp.concatenate([sibling, down], axis=1)
            down = dot(both, wdn[2 * u + side]).astype(BF16)
            u -= 1

    whole = dot(down, wsel[...])
    for s in range(2):
        child = whole[:, 128 * s : 128 * s + 128]
        nodes[s] = jnp.where(lanes[0:16], child[0:16], child[16:32]).astype(BF16)
    at, m = 0, 2
    while m < OWN:
        whole = jnp.concatenate([nodes[at + j] for j in range(m)], axis=0)
        child = dot(whole, wld[...]).astype(BF16)
        for j in range(m):
            for s in range(2):
                nodes[at + m + 2 * j + s] = child[
                    16 * j : 16 * j + 16, 128 * s : 128 * s + 128
                ]
        at, m = at + m, 2 * m
    whole = jnp.concatenate([nodes[at + j] for j in range(OWN)], axis=0)
    for h in range(2):
        low = dot(whole, wleaf[h])
        for j in range(OWN):
            for s in range(2):
                ldown[2 * j + s, pl.ds(16 * h, 16), :] = low[
                    16 * j : 16 * j + 16, 128 * s : 128 * s + 128
                ]

    sl.wait_recv()
    ln.wait()
    so.wait_recv()

    @pl.loop(0, 32, step=8)
    def _(i0):
        for k in range(8):
            i = i0 + k
            leaf_local = (yfar[i] + ldown[i][:, 0:64]).astype(BF16)
            out[:, cols(i)] += dot(leaf_local, bx[i])

    for copy in (sv, sb, sl, sr, sc, se0, se1, sn, ss, so):
        copy.wait_send()

    @pl.when(c == 0)
    def _():
        sp.wait_send()
        st.wait_send()

    for stage in stages:

        @pl.loop(1, stage[1])
        def _(t):
            ring(stage, t).wait_send()


def solution(mesh):
    n = mesh.shape["leaf"]
    dims = (4, 4, 8) if n == 128 else (2, 2, n // 4)
    yn, xn, zn = dims
    upl = (n - 1).bit_length()
    hbm = pl.BlockSpec(memory_space=pltpu.HBM)
    vmem = pl.BlockSpec(memory_space=pltpu.VMEM)
    smem = pl.BlockSpec(memory_space=pltpu.SMEM)
    dma = pltpu.SemaphoreType.DMA

    def on_device(values, points, basis, near_list, far_list, *rest):
        return pl.pallas_call(
            functools.partial(kernel, dims),
            out_shape=pltpu.VMEM((32, 8192), F32),
            in_specs=[hbm, hbm, hbm, vmem, smem, smem, hbm, vmem, vmem, vmem],
            out_specs=vmem,
            scratch_shapes=[
                pltpu.VMEM((64, EXT * LEAF), BF16),
                pltpu.VMEM((3, EXT * LEAF), F32),
                pltpu.VMEM((32, EXT * LEAF), BF16),
                pltpu.VMEM((32, EXT * LEAF), BF16),
                pltpu.VMEM((32, 64, LEAF), BF16),
                pltpu.VMEM((32, 8, 64, 64), BF16),
                pltpu.VMEM((OWN, LEAF, (HW + 1) * LEAF), BF16),
                pltpu.VMEM((64, EXT * LEAF), F32),
                pltpu.VMEM((OWN, 64, 128), BF16),
                pltpu.VMEM((41, 32, 128), BF16),
                pltpu.VMEM((31, 32, 128), BF16),
                pltpu.VMEM((32, 32, 128), F32),
                pltpu.VMEM((32, 32, 64), F32),
                pltpu.VMEM((30, 16, 128), BF16),
                pltpu.VMEM((2, 32, 128), BF16),
                pltpu.VMEM((2 * zn, 32, 128), BF16),
                pltpu.VMEM((2 * xn, 32, 128), BF16),
                pltpu.VMEM((2 * yn, 32, 128), BF16),
                pltpu.VMEM((upl, 256, 128), BF16),
                pltpu.VMEM((2 * upl, 256, 128), BF16),
                pltpu.VMEM((128, 256), BF16),
                pltpu.VMEM((128, 256), BF16),
                pltpu.VMEM((2, 128, 256), BF16),
                pltpu.VMEM((16, 128), F32),
                pltpu.VMEM((16, 128), F32),
                pltpu.SMEM((16, 128), F32),
                pltpu.SMEM((16, 128), F32),
                pltpu.VMEM((64, HW * LEAF), F32),
                dma((8,)),
                dma((12,)),
                dma((13,)),
                dma((zn - 1,)),
                dma((zn - 1,)),
                dma((xn - 1,)),
                dma((xn - 1,)),
                dma((yn - 1,)),
                dma((yn - 1,)),
            ],
            compiler_params=pltpu.CompilerParams(
                collective_id=0, has_side_effects=True, vmem_limit_bytes=56 * 2**20
            ),
            name="h2_matvec",
        )(values, points, basis, near_list.T, far_list.T, *rest)

    placed = (
        P("rhs", "leaf"),
        P(None, "leaf"),
        P("leaf", "rhs", None),
        P("leaf", None),
        P("leaf", None),
        P("leaf"),
        P("leaf", None, None, None),
        P(),
        P(),
        P(),
    )
    return jax.shard_map(
        on_device, mesh=mesh, in_specs=placed, out_specs=P("rhs", "leaf"), check_vma=False
    )
```

```python
import functools
import math

import jax
import jax.numpy as jnp
import numpy as np
from jax import lax
from jax.experimental import pallas as pl
from jax.experimental.pallas import tpu as pltpu
from jax.sharding import PartitionSpec as P

MESH = pl.DeviceIdType.MESH
F32 = jnp.float32
BF16 = jnp.bfloat16
HW = 4
WAVE = 20.0
SMOOTH = 0.05
LEAF = 256
OWN = 16
EXT = OWN + 2 * HW
SCALE = WAVE / (2 * math.pi)
SOFT = SCALE * SCALE * SMOOTH * SMOOTH
DEGREE = 4
SCHEDULE = (
    (5, 0, 0, 5, 10, 0),
    (4, 0, 0, 4, 10, 1),
    (3, 0, 0, 4, 10, 1),
    (3, 0, 0, 4, 10, 1),
    (2, 0, 0, 4, 10, 1),
    (1, 1, 1, 5, 10, 1),
)


def cosine_fit():
    nodes = 0.125 + 0.125 * np.cos(np.pi * (np.arange(64) + 0.5) / 64)
    series = np.polynomial.chebyshev.Chebyshev.fit(
        nodes, np.cos(2 * np.pi * np.sqrt(nodes)), DEGREE, domain=[0, 0.25]
    )
    return [float(v) for v in series.convert(kind=np.polynomial.Polynomial).coef]


COSINE = cosine_fit()
FACTOR = COSINE[DEGREE] * SCALE / math.sqrt(9 * LEAF)


def entries(scaled):
    scaled = jnp.maximum(scaled, 1e-12)
    turns = scaled * lax.rsqrt(scaled)
    rest = turns - jnp.round(turns)
    square = rest * rest
    poly = square + COSINE[DEGREE - 1] / COSINE[DEGREE]
    for power in range(DEGREE - 2, -1, -1):
        poly = poly * square + COSINE[power] / COSINE[DEGREE]
    return (poly * lax.rsqrt(scaled + SOFT)).astype(BF16)


def dot(a, b, left=1, right=0):
    return lax.dot_general(a, b, (((left,), (right,)), ((), ())), preferred_element_type=F32)


def cols(leaf, count=1):
    return pl.ds(pl.multiple_of(leaf * LEAF, LEAF), count * LEAF)


def diagonal(block):
    block = block.astype(F32)
    zero = jnp.zeros_like(block)
    top = jnp.concatenate([block, zero], axis=1)
    low = jnp.concatenate([zero, block], axis=1)
    return jnp.concatenate([top, low], axis=0).astype(BF16)


def kernel(
    dims,
    values,
    points,
    basis,
    near_list,
    far_list,
    far_count,
    couple,
    local_transfer,
    upper_transfer,
    upper_couple,
    out,
    vx,
    px,
    fa,
    fb,
    bx,
    cv,
    kb,
    acc,
    dco,
    fco,
    lev,
    ldown,
    yfar,
    nodes,
    pair,
    zb,
    xb,
    yb,
    wup,
    wdn,
    wld,
    wroot,
    wleaf,
    tally,
    tally_next,
    count,
    count_next,
    spill,
    loc,
    ssem,
    rsem,
    zs,
    zr,
    xs,
    xr,
    ys,
    yr,
):
    yn, xn, zn = dims
    n = yn * xn * zn
    d = lax.axis_index("leaf")
    c = lax.axis_index("rhs")
    p = 1 - c
    z = lax.rem(d, zn)
    x = lax.rem(d // zn, xn)
    y = d // (zn * xn)
    after = lax.rem(d + 1, n)
    before = lax.rem(d + n - 1, n)
    beside = lax.rem(d + n - 1 + 2 * c, n)
    upl = (n - 1).bit_length()
    own = pl.ds(32 * c, 32)

    barrier = pltpu.get_barrier_semaphore()

    def greet(leaf, core):
        pl.semaphore_signal(barrier, inc=1, device_id=(leaf, core), device_id_type=MESH)

    def z_peer(t):
        return d - z + lax.rem(z + t, zn)

    def x_peer(t):
        return d + (lax.rem(x + t, xn) - x) * zn

    def y_peer(t):
        return d + (lax.rem(y + t, yn) - y) * zn * xn

    stages = (
        (zb, zn, z, zs, zr, z_peer),
        (xb, xn, x, xs, xr, x_peer),
        (yb, yn, y, ys, yr, y_peer),
    )

    greet(d, p)
    greet(before, 1)
    greet(after, 0)

    @pl.when(c == 1)
    def _():
        greet(after, 1)

    for _, size, _, _, _, peer in stages:

        @pl.loop(1, size)
        def _(t):
            greet(peer(t), c)

    def local(src, dst, k):
        return pltpu.make_async_copy(src, dst, loc.at[k])

    lp = local(points.at[:, cols(12 * c, 20)], px.at[:, cols(4 - 4 * c, 20)], 0)
    lv = local(
        values.at[:, cols(12 * c, 20)], vx.at[own, cols(4 - 4 * c, 20)], 1
    )
    lb = local(basis, bx.at[:, own, :], 2)
    lc = local(couple, cv, 3)
    lf = local(dco.at[:, own, :], fco.at[pl.ds(16 * c + HW, OWN)], 4)
    lt = local(tally, count, 6)
    lu = local(tally_next, count_next, 7)
    ln = local(acc.at[own, cols(HW, OWN)], out.at[:, cols(16 * c, OWN)], 5)
    for copy in (lp, lv, lb, lc):
        copy.start()

    def remote(src, dst, k, r, leaf, core):
        return pltpu.make_async_remote_copy(
            src_ref=src,
            dst_ref=dst,
            send_sem=ssem.at[k],
            recv_sem=rsem.at[r],
            device_id=(leaf, core),
            device_id_type=MESH,
        )

    sv = remote(values.at[:, cols(12 * p, 20)], vx.at[own, cols(4 - 4 * p, 20)], 0, 0, d, p)
    sb = remote(
        basis.at[pl.ds(16 * p, 16)], bx.at[pl.ds(16 * p, 16), own, :], 1, 1, d, p
    )
    sl = remote(
        basis.at[pl.ds(16 * c, 16)], bx.at[pl.ds(16 * c, 16), own, :], 2, 2, d, p
    )
    sp = remote(points.at[:, cols(0, 4)], px.at[:, cols(20, 4)], 3, 3, before, 1)
    st = remote(tally, tally_next, 4, 11, before, 1)
    sr = remote(values.at[:, cols(0, 4)], vx.at[own, cols(20, 4)], 5, 4 + c, before, 1)
    ss = remote(
        acc.at[:, cols(20, 4)], spill, 11, 12, lax.rem(d + c, n), p
    )
    sc = remote(
        dco.at[:, pl.ds(32 * p, 32), :], fco.at[pl.ds(16 * c + HW, OWN)], 6, 6, d, p
    )
    se0, se1 = [
        remote(
            dco.at[pl.ds(12 * c, HW), pl.ds(32 * q, 32), :],
            fco.at[pl.ds(36 * p, HW)],
            7 + q,
            7 + c,
            beside,
            q,
        )
        for q in range(2)
    ]
    sn = remote(lev.at[30], pair.at[c], 9, 9, d, p)
    so = remote(
        acc.at[pl.ds(32 * p, 32), cols(HW, OWN)], out.at[:, cols(16 * c, OWN)], 10, 10, d, p
    )

    def arrived(ref, r):
        pltpu.make_async_copy(ref, ref, rsem.at[r]).wait()

    def ring(stage, t):
        buf, size, me, sems, recvs, peer = stage
        return pltpu.make_async_remote_copy(
            src_ref=buf.at[me],
            dst_ref=buf.at[me],
            send_sem=sems.at[t - 1],
            recv_sem=recvs.at[t - 1],
            device_id=(peer(t), c),
            device_id_type=MESH,
        )

    def ring_start(stage):
        @pl.loop(1, stage[1])
        def _(t):
            ring(stage, t).start()

    def ring_recv(stage):
        @pl.loop(1, stage[1])
        def _(t):
            ring(stage, t).wait_recv()

    def weights():
        zero = jnp.zeros((64, 64), F32)
        none = jnp.zeros((64, 128), BF16)
        for s in range(2):
            t = local_transfer[s]
            wup[0, pl.ds(128 * s, 128), :] = diagonal(t)
            td = t.astype(F32).T
            wld[:, pl.ds(128 * s, 128)] = diagonal(td)
            tf = t.astype(F32)
            wroot[pl.ds(128 * s + 64 * c, 64), :] = jnp.concatenate(
                [tf, tf], axis=1
            ).astype(BF16)
            wroot[pl.ds(128 * s + 64 * p, 64), :] = none
            wide = jnp.concatenate([td, zero], axis=1).astype(BF16)
            wleaf[0, pl.ds(0, 64), pl.ds(128 * s, 128)] = wide
            wleaf[0, pl.ds(64, 64), pl.ds(128 * s, 128)] = none
            wleaf[1, pl.ds(0, 64), pl.ds(128 * s, 128)] = none
            wleaf[1, pl.ds(64, 64), pl.ds(128 * s, 128)] = wide
        for u in range(upl):
            for s in range(2):
                t = upper_transfer[u, s]
                if u < upl - 1:
                    wup[u + 1, pl.ds(128 * s, 128), :] = diagonal(t)
                wdn[2 * u + s, pl.ds(0, 128), :] = diagonal(upper_couple[u, s])
                wdn[2 * u + s, pl.ds(128, 128), :] = diagonal(t.astype(F32).T)

    def counts():
        leaf = lax.broadcasted_iota(jnp.int32, (9, 32), 1)
        offset = near_list[...] - leaf - d * 32
        tally[...] = jnp.zeros_like(tally)
        for o in range(9):
            same = jnp.where(offset == o - HW, FACTOR, 0.0)
            tally[pl.ds(o, 1), pl.ds(0, 32)] = jnp.sum(same, axis=0, keepdims=True)
        lt.start()

    def often(i, o):
        row = 16 * c + i
        return jnp.where(
            row < 32, count[o, row], count_next[o, jnp.maximum(row - 32, 0)]
        )

    rows = lax.broadcasted_iota(jnp.int32, (8, LEAF), 0)

    def factors(e):
        at = cols(e)
        pts = (px[:, at] - 0.5) * SCALE
        pts = jnp.concatenate([pts, jnp.zeros((5, LEAF), F32)], axis=0)
        high = pts.astype(BF16).astype(F32)
        low = (pts - high).astype(BF16).astype(F32)
        both = high + low
        norm = jnp.sum(both * both, axis=0, keepdims=True)
        n1 = norm.astype(BF16).astype(F32)
        n2 = (norm - n1).astype(BF16).astype(F32)
        n3 = (norm - n1 - n2).astype(BF16).astype(F32)
        norms = jnp.where(
            rows == 3, n1, jnp.where(rows == 4, n2, jnp.where(rows == 5, n3, 0.0))
        )
        ones = jnp.where((rows >= 3) & (rows <= 5), 1.0, 0.0)
        fa[:, at] = jnp.concatenate([high + norms, high + ones, low, low], axis=0).astype(BF16)
        fb[:, at] = jnp.concatenate(
            [ones - 2 * high, norms - 2 * low, -2 * high, -2 * low], axis=0
        ).astype(BF16)

    def kernel_row(q):
        left = fa[:, cols(q + HW)]
        own_right = fb[:, cols(q + HW)]
        top = entries(dot(left[:, 0:128], own_right, 0, 0))
        low = entries(dot(left[:, 128:256], own_right[:, 128:256], 0, 0))
        kb[q, pl.ds(0, 128), pl.ds(0, LEAF)] = top
        kb[q, pl.ds(128, 128), pl.ds(128, 128)] = low
        kb[q, pl.ds(128, 128), pl.ds(0, 128)] = top[:, 128:256].T
        for b in range(1, HW + 1):
            kb[q, :, pl.ds(b * LEAF, LEAF)] = entries(dot(left, fb[:, cols(q + HW + b)], 0, 0))

    def near_main(i):
        e = i + HW
        mine = vx[:, cols(e)]
        total = None
        parts = []
        for o in range(HW + 1):
            block = kb[i, :, pl.ds(o * LEAF, LEAF)]
            term = dot(vx[:, cols(e + o)], block, 1, 1) * often(i, HW + o)
            total = term if total is None else total + term
            if o:
                parts.append(dot(mine, block, 1, 0) * often(i + o, HW - o))
        acc[:, cols(e, HW + 1)] += jnp.concatenate([total] + parts, axis=1)

    def joined(read, m):
        return jnp.concatenate(
            [jnp.concatenate([read(2 * j), read(2 * j + 1)], axis=1) for j in range(m)], axis=0
        )

    def upward(src, at, dst, to, m, weight):
        high = src.shape[1]
        whole = dot(joined(lambda j: src[at + j], m), wup[weight]).astype(BF16)
        for j in range(m):
            dst[to + j] = whole[high * j : high * j + high]

    def levels(stage, weight):
        buf, size = stage[:2]
        at, m = 0, size
        while m > 2:
            upward(buf, at, buf, at + m, m // 2, weight)
            at, m, weight = at + m, m // 2, weight + 1
        return at, weight

    def merged(stage, weight):
        at, weight = levels(stage, weight)
        return dot(joined(lambda j: stage[0][at + j], 1), wup[weight]).astype(BF16)

    def depth(size):
        return (size - 1).bit_length()

    def enter():
        pl.semaphore_wait(barrier, 3 + c + (zn - 1) + (xn - 1) + (yn - 1))
        for copy in (sb, sv):
            copy.start()

        @pl.when(c == 0)
        def _():
            sp.start()
            st.start()

        sr.start()
        sl.start()
        weights()

    lanes = lax.broadcasted_iota(jnp.int32, (32, 128), 1) < 64

    def coefficients():
        lv.wait()
        sv.wait_recv()
        lb.wait()
        sb.wait_recv()
        lt.wait()

        @pl.loop(0, OWN, step=8)
        def _(i0):
            for k in range(8):
                i = i0 + k
                mine = bx[16 * c + i]
                full = dot(
                    vx[:, cols(i + HW)], jnp.concatenate([mine, mine], axis=0), 1, 1
                )
                dco[i] = full.astype(BF16)
                lev[i] = jnp.where(lanes, full[0:32], full[32:64]).astype(BF16)

        upward(lev, 0, lev, 16, 8, 0)
        upward(lev, 16, lev, 24, 4, 0)
        upward(lev, 24, lev, 28, 2, 0)
        whole = dot(joined(lambda j: lev[28 + j], 1), wup[0]).astype(BF16)
        lev[30] = whole
        pair[c] = whole
        sn.start()
        for copy in (sc, se0, se1, lf):
            copy.start()

    def z_stage():
        sn.wait_recv()
        root = dot(joined(lambda j: pair[j], 1), wroot[...])
        zb[z] = jnp.where(lanes[0:16], root[0:16], root[16:32]).astype(BF16)
        ring_start(stages[0])

    def x_stage():
        ring_recv(stages[0])
        xb[x] = merged(stages[0], 1)
        ring_start(stages[1])

    def y_stage():
        ring_recv(stages[1])
        yb[y] = merged(stages[1], 1 + depth(zn))
        ring_start(stages[2])

    def rims():
        @pl.when(c == 1)
        def _():
            sp.wait_recv()
            for r in range(2):
                arrived(vx.at[pl.ds(0, 32), cols(20, 4)], 4 + r)
            st.wait_recv()
            lu.start()
            for e in range(4):
                factors(e + 20)
            lu.wait()

    def place(k):
        at = SCHEDULE[-1][k]
        for row in range(1, len(SCHEDULE) - 1):
            at = jnp.where(z == row - 1, SCHEDULE[row][k], at)
        return jnp.where(d == 0, SCHEDULE[0][k], at)

    ahead = place(0)
    last = place(5)
    events = tuple(
        (place(k + 1), event)
        for k, event in enumerate((coefficients, z_stage, x_stage, y_stage))
    ) + ((last, rims), (last + HW + 2, ss.start))

    lp.wait()

    @pl.loop(0, 20, step=4)
    def _(e):
        for k in range(4):
            factors(e + k + 4 - 4 * c)

    acc[...] = jnp.zeros_like(acc)
    fco[40] = jnp.zeros((32, 128), BF16)
    counts()

    @pl.loop(0, ahead)
    def _(t):
        kernel_row(2 * t)
        kernel_row(2 * t + 1)

    enter()

    @pl.loop(0, 24 - 2 * ahead)
    def _(t):
        for when, event in events:
            pl.when(t == when)(event)
        left = 18 - 2 * ahead
        here = t - last
        kernels = (here < HW) | ((here >= HW + 2) & (t < left))

        @pl.when(kernels)
        def _():
            row = jnp.where(here < HW, here + 12, 2 * ahead + t - HW - 2)
            kernel_row(jnp.where(here < 0, 2 * ahead + t, row))

        @pl.when(jnp.logical_not(kernels))
        def _():
            i = 2 * jnp.where(t < left, here + 2, t - left)
            near_main(i)
            near_main(i + 1)

    ss.wait_recv()
    acc[:, cols(HW, HW)] += spill[...]
    so.start()
    ln.start()

    lf.wait()
    sc.wait_recv()
    for r in range(2):
        arrived(fco.at[pl.ds(0, HW)], 7 + r)
    lc.wait()
    pick0 = jnp.where(lanes, 1.0, 0.0).astype(BF16)
    pick1 = jnp.where(lanes, 0.0, 1.0).astype(BF16)

    @pl.loop(0, 32, step=4)
    def _(i0):
        for k in range(4):
            i = i0 + k
            used = far_count[i]
            at = [jnp.where(s < used, far_list[s, i] - d * 32 + HW, 40) for s in range(8)]
            coeffs = jnp.concatenate(
                [fco[at[2 * q]] * pick0 + fco[at[2 * q + 1]] * pick1 for q in range(4)], axis=1
            )
            yfar[i] = dot(coeffs, cv[i].reshape(512, 64))

    ring_recv(stages[2])
    levels(stages[2], 1 + depth(zn) + depth(xn))

    down = jnp.zeros((16, 128), BF16)
    u = upl - 1
    for buf, size, me, _, _, _ in reversed(stages):
        for step in range(depth(size) - 1, -1, -1):
            here = me // 2**step
            side = lax.rem(here, 2)
            sibling = buf[2 * size - 2 * (size >> step) + here + 1 - 2 * side]
            both = jnp.concatenate([sibling, down], axis=1)
            down = dot(both, wdn[2 * u + side]).astype(BF16)
            u -= 1

    nodes[0] = down
    at, m = 0, 1
    while m < OWN:
        whole = jnp.concatenate([nodes[at + j] for j in range(m)], axis=0)
        child = dot(whole, wld[...]).astype(BF16)
        for j in range(m):
            for s in range(2):
                nodes[at + m + 2 * j + s] = child[
                    16 * j : 16 * j + 16, 128 * s : 128 * s + 128
                ]
        at, m = at + m, 2 * m
    whole = jnp.concatenate([nodes[at + j] for j in range(OWN)], axis=0)
    for h in range(2):
        low = dot(whole, wleaf[h])
        for j in range(OWN):
            for s in range(2):
                ldown[2 * j + s, pl.ds(16 * h, 16), :] = low[
                    16 * j : 16 * j + 16, 128 * s : 128 * s + 128
                ]

    sl.wait_recv()
    ln.wait()
    so.wait_recv()

    @pl.loop(0, 32, step=8)
    def _(i0):
        for k in range(8):
            i = i0 + k
            leaf_local = (yfar[i] + ldown[i][:, 0:64]).astype(BF16)
            out[:, cols(i)] += dot(leaf_local, bx[i])

    for copy in (sv, sb, sl, sr, sc, se0, se1, sn, ss, so):
        copy.wait_send()

    @pl.when(c == 0)
    def _():
        sp.wait_send()
        st.wait_send()

    for stage in stages:

        @pl.loop(1, stage[1])
        def _(t):
            ring(stage, t).wait_send()


def solution(mesh):
    n = mesh.shape["leaf"]
    dims = (4, 4, 8) if n == 128 else (2, 2, n // 4)
    yn, xn, zn = dims
    upl = (n - 1).bit_length()
    hbm = pl.BlockSpec(memory_space=pltpu.HBM)
    vmem = pl.BlockSpec(memory_space=pltpu.VMEM)
    smem = pl.BlockSpec(memory_space=pltpu.SMEM)
    dma = pltpu.SemaphoreType.DMA

    def on_device(values, points, basis, near_list, far_list, *rest):
        return pl.pallas_call(
            functools.partial(kernel, dims),
            out_shape=pltpu.VMEM((32, 8192), F32),
            in_specs=[hbm, hbm, hbm, vmem, smem, smem, hbm, vmem, vmem, vmem],
            out_specs=vmem,
            scratch_shapes=[
                pltpu.VMEM((64, EXT * LEAF), BF16),
                pltpu.VMEM((3, EXT * LEAF), F32),
                pltpu.VMEM((32, EXT * LEAF), BF16),
                pltpu.VMEM((32, EXT * LEAF), BF16),
                pltpu.VMEM((32, 64, LEAF), BF16),
                pltpu.VMEM((32, 8, 64, 64), BF16),
                pltpu.VMEM((OWN, LEAF, (HW + 1) * LEAF), BF16),
                pltpu.VMEM((64, EXT * LEAF), F32),
                pltpu.VMEM((OWN, 64, 128), BF16),
                pltpu.VMEM((41, 32, 128), BF16),
                pltpu.VMEM((31, 32, 128), BF16),
                pltpu.VMEM((32, 32, 128), F32),
                pltpu.VMEM((32, 32, 64), F32),
                pltpu.VMEM((31, 16, 128), BF16),
                pltpu.VMEM((2, 32, 128), BF16),
                pltpu.VMEM((2 * zn, 16, 128), BF16),
                pltpu.VMEM((2 * xn, 16, 128), BF16),
                pltpu.VMEM((2 * yn, 16, 128), BF16),
                pltpu.VMEM((upl, 256, 128), BF16),
                pltpu.VMEM((2 * upl, 256, 128), BF16),
                pltpu.VMEM((128, 256), BF16),
                pltpu.VMEM((256, 128), BF16),
                pltpu.VMEM((2, 128, 256), BF16),
                pltpu.VMEM((16, 128), F32),
                pltpu.VMEM((16, 128), F32),
                pltpu.SMEM((16, 128), F32),
                pltpu.SMEM((16, 128), F32),
                pltpu.VMEM((64, HW * LEAF), F32),
                dma((8,)),
                dma((12,)),
                dma((13,)),
                dma((zn - 1,)),
                dma((zn - 1,)),
                dma((xn - 1,)),
                dma((xn - 1,)),
                dma((yn - 1,)),
                dma((yn - 1,)),
            ],
            compiler_params=pltpu.CompilerParams(
                collective_id=0, has_side_effects=True, vmem_limit_bytes=56 * 2**20
            ),
            name="h2_matvec",
        )(values, points, basis, near_list.T, far_list.T, *rest)

    placed = (
        P("rhs", "leaf"),
        P(None, "leaf"),
        P("leaf", "rhs", None),
        P("leaf", None),
        P("leaf", None),
        P("leaf"),
        P("leaf", None, None, None),
        P(),
        P(),
        P(),
    )
    return jax.shard_map(
        on_device, mesh=mesh, in_specs=placed, out_specs=P("rhs", "leaf"), check_vma=False
    )
```

```python
import functools
import math

import jax
import jax.numpy as jnp
import numpy as np
from jax import lax
from jax.experimental import pallas as pl
from jax.experimental.pallas import tpu as pltpu
from jax.sharding import PartitionSpec as P

MESH = pl.DeviceIdType.MESH
F32 = jnp.float32
BF16 = jnp.bfloat16
HW = 4
WAVE = 20.0
SMOOTH = 0.05
LEAF = 256
OWN = 16
EXT = OWN + 2 * HW
SCALE = WAVE / (2 * math.pi)
SOFT = SCALE * SCALE * SMOOTH * SMOOTH
DEGREE = 4
SCHEDULE = (
    (4, 0, 0, 4, 9, 0),
    (3, 0, 0, 4, 9, 1),
    (2, 0, 0, 4, 9, 1),
    (2, 0, 0, 4, 9, 1),
    (1, 0, 0, 4, 9, 1),
    (1, 0, 0, 5, 9, 1),
)


def cosine_fit():
    nodes = 0.125 + 0.125 * np.cos(np.pi * (np.arange(64) + 0.5) / 64)
    series = np.polynomial.chebyshev.Chebyshev.fit(
        nodes, np.cos(2 * np.pi * np.sqrt(nodes)), DEGREE, domain=[0, 0.25]
    )
    return [float(v) for v in series.convert(kind=np.polynomial.Polynomial).coef]


COSINE = cosine_fit()
FACTOR = COSINE[DEGREE] * SCALE / math.sqrt(9 * LEAF)


def entries(scaled):
    scaled = jnp.maximum(scaled, 1e-12)
    turns = scaled * lax.rsqrt(scaled)
    rest = turns - jnp.round(turns)
    square = rest * rest
    poly = square + COSINE[DEGREE - 1] / COSINE[DEGREE]
    for power in range(DEGREE - 2, -1, -1):
        poly = poly * square + COSINE[power] / COSINE[DEGREE]
    return (poly * lax.rsqrt(scaled + SOFT)).astype(BF16)


def dot(a, b, left=1, right=0):
    return lax.dot_general(a, b, (((left,), (right,)), ((), ())), preferred_element_type=F32)


def cols(leaf, count=1):
    return pl.ds(pl.multiple_of(leaf * LEAF, LEAF), count * LEAF)


def diagonal(block):
    block = block.astype(F32)
    zero = jnp.zeros_like(block)
    top = jnp.concatenate([block, zero], axis=1)
    low = jnp.concatenate([zero, block], axis=1)
    return jnp.concatenate([top, low], axis=0).astype(BF16)


def kernel(
    dims,
    values,
    points,
    basis,
    near_list,
    far_list,
    far_count,
    couple,
    local_transfer,
    upper_transfer,
    upper_couple,
    out,
    vx,
    px,
    fa,
    fb,
    bx,
    cv,
    kb,
    acc,
    dco,
    fco,
    lev,
    ldown,
    yfar,
    nodes,
    pair,
    zb,
    xb,
    yb,
    wup,
    wdn,
    wld,
    wroot,
    wleaf,
    tally,
    tally_next,
    count,
    count_next,
    spill,
    loc,
    ssem,
    rsem,
    zs,
    zr,
    xs,
    xr,
    ys,
    yr,
):
    yn, xn, zn = dims
    n = yn * xn * zn
    d = lax.axis_index("leaf")
    c = lax.axis_index("rhs")
    p = 1 - c
    z = lax.rem(d, zn)
    x = lax.rem(d // zn, xn)
    y = d // (zn * xn)
    after = lax.rem(d + 1, n)
    before = lax.rem(d + n - 1, n)
    beside = lax.rem(d + n - 1 + 2 * c, n)
    upl = (n - 1).bit_length()
    own = pl.ds(32 * c, 32)

    barrier = pltpu.get_barrier_semaphore()

    def greet(leaf, core):
        pl.semaphore_signal(barrier, inc=1, device_id=(leaf, core), device_id_type=MESH)

    def z_peer(t):
        return d - z + lax.rem(z + t, zn)

    def x_peer(t):
        return d + (lax.rem(x + t, xn) - x) * zn

    def y_peer(t):
        return d + (lax.rem(y + t, yn) - y) * zn * xn

    stages = (
        (zb, zn, z, zs, zr, z_peer),
        (xb, xn, x, xs, xr, x_peer),
        (yb, yn, y, ys, yr, y_peer),
    )

    greet(d, p)
    greet(before, 1)
    greet(after, 0)

    @pl.when(c == 1)
    def _():
        greet(after, 1)

    for _, size, _, _, _, peer in stages:

        @pl.loop(1, size)
        def _(t):
            greet(peer(t), c)

    def local(src, dst, k):
        return pltpu.make_async_copy(src, dst, loc.at[k])

    lp = local(points.at[:, cols(12 * c, 20)], px.at[:, cols(4 - 4 * c, 20)], 0)
    lv = local(
        values.at[:, cols(12 * c, 20)], vx.at[own, cols(4 - 4 * c, 20)], 1
    )
    lb = local(basis, bx.at[:, own, :], 2)
    lc = local(couple, cv, 3)
    lf = local(dco.at[:, own, :], fco.at[pl.ds(16 * c + HW, OWN)], 4)
    lt = local(tally, count, 6)
    lu = local(tally_next, count_next, 7)
    ln = local(acc.at[own, cols(HW, OWN)], out.at[:, cols(16 * c, OWN)], 5)
    for copy in (lp, lv, lb, lc):
        copy.start()

    def remote(src, dst, k, r, leaf, core):
        return pltpu.make_async_remote_copy(
            src_ref=src,
            dst_ref=dst,
            send_sem=ssem.at[k],
            recv_sem=rsem.at[r],
            device_id=(leaf, core),
            device_id_type=MESH,
        )

    sv = remote(values.at[:, cols(12 * p, 20)], vx.at[own, cols(4 - 4 * p, 20)], 0, 0, d, p)
    sb = remote(
        basis.at[pl.ds(16 * p, 16)], bx.at[pl.ds(16 * p, 16), own, :], 1, 1, d, p
    )
    sl = remote(
        basis.at[pl.ds(16 * c, 16)], bx.at[pl.ds(16 * c, 16), own, :], 2, 2, d, p
    )
    sp = remote(points.at[:, cols(0, 4)], px.at[:, cols(20, 4)], 3, 3, before, 1)
    st = remote(tally, tally_next, 4, 11, before, 1)
    sr = remote(values.at[:, cols(0, 4)], vx.at[own, cols(20, 4)], 5, 4 + c, before, 1)
    ss = remote(
        acc.at[:, cols(20, 4)], spill, 11, 12, lax.rem(d + c, n), p
    )
    sc = remote(
        dco.at[:, pl.ds(32 * p, 32), :], fco.at[pl.ds(16 * c + HW, OWN)], 6, 6, d, p
    )
    se0, se1 = [
        remote(
            dco.at[pl.ds(12 * c, HW), pl.ds(32 * q, 32), :],
            fco.at[pl.ds(36 * p, HW)],
            7 + q,
            7 + c,
            beside,
            q,
        )
        for q in range(2)
    ]
    sn = remote(lev.at[30], pair.at[c], 9, 9, d, p)
    so = remote(
        acc.at[pl.ds(32 * p, 32), cols(HW, OWN)], out.at[:, cols(16 * c, OWN)], 10, 10, d, p
    )

    def arrived(ref, r):
        pltpu.make_async_copy(ref, ref, rsem.at[r]).wait()

    def ring(stage, t):
        buf, size, me, sems, recvs, peer = stage
        return pltpu.make_async_remote_copy(
            src_ref=buf.at[me],
            dst_ref=buf.at[me],
            send_sem=sems.at[t - 1],
            recv_sem=recvs.at[t - 1],
            device_id=(peer(t), c),
            device_id_type=MESH,
        )

    def ring_start(stage):
        @pl.loop(1, stage[1])
        def _(t):
            ring(stage, t).start()

    def ring_recv(stage):
        @pl.loop(1, stage[1])
        def _(t):
            ring(stage, t).wait_recv()

    def weights():
        zero = jnp.zeros((64, 64), F32)
        none = jnp.zeros((64, 128), BF16)
        for s in range(2):
            t = local_transfer[s]
            wup[0, pl.ds(128 * s, 128), :] = diagonal(t)
            td = t.astype(F32).T
            wld[:, pl.ds(128 * s, 128)] = diagonal(td)
            tf = t.astype(F32)
            wroot[pl.ds(128 * s + 64 * c, 64), :] = jnp.concatenate(
                [tf, tf], axis=1
            ).astype(BF16)
            wroot[pl.ds(128 * s + 64 * p, 64), :] = none
            wide = jnp.concatenate([td, zero], axis=1).astype(BF16)
            wleaf[0, pl.ds(0, 64), pl.ds(128 * s, 128)] = wide
            wleaf[0, pl.ds(64, 64), pl.ds(128 * s, 128)] = none
            wleaf[1, pl.ds(0, 64), pl.ds(128 * s, 128)] = none
            wleaf[1, pl.ds(64, 64), pl.ds(128 * s, 128)] = wide
        for u in range(upl):
            for s in range(2):
                t = upper_transfer[u, s]
                if u < upl - 1:
                    wup[u + 1, pl.ds(128 * s, 128), :] = diagonal(t)
                wdn[2 * u + s, pl.ds(0, 128), :] = diagonal(upper_couple[u, s])
                wdn[2 * u + s, pl.ds(128, 128), :] = diagonal(t.astype(F32).T)

    def counts():
        leaf = lax.broadcasted_iota(jnp.int32, (9, 32), 1)
        offset = near_list[...] - leaf - d * 32
        tally[...] = jnp.zeros_like(tally)
        for o in range(9):
            same = jnp.where(offset == o - HW, FACTOR, 0.0)
            tally[pl.ds(o, 1), pl.ds(0, 32)] = jnp.sum(same, axis=0, keepdims=True)
        lt.start()

    def often(i, o):
        row = 16 * c + i
        return jnp.where(
            row < 32, count[o, row], count_next[o, jnp.maximum(row - 32, 0)]
        )

    rows = lax.broadcasted_iota(jnp.int32, (8, LEAF), 0)

    def factors(e):
        at = cols(e)
        pts = (px[:, at] - 0.5) * SCALE
        pts = jnp.concatenate([pts, jnp.zeros((5, LEAF), F32)], axis=0)
        high = pts.astype(BF16).astype(F32)
        low = (pts - high).astype(BF16).astype(F32)
        both = high + low
        norm = jnp.sum(both * both, axis=0, keepdims=True)
        n1 = norm.astype(BF16).astype(F32)
        n2 = (norm - n1).astype(BF16).astype(F32)
        n3 = (norm - n1 - n2).astype(BF16).astype(F32)
        norms = jnp.where(
            rows == 3, n1, jnp.where(rows == 4, n2, jnp.where(rows == 5, n3, 0.0))
        )
        ones = jnp.where((rows >= 3) & (rows <= 5), 1.0, 0.0)
        fa[:, at] = jnp.concatenate([high + norms, high + ones, low, low], axis=0).astype(BF16)
        fb[:, at] = jnp.concatenate(
            [ones - 2 * high, norms - 2 * low, -2 * high, -2 * low], axis=0
        ).astype(BF16)

    def kernel_row(q):
        left = fa[:, cols(q + HW)]
        own_right = fb[:, cols(q + HW)]
        top = entries(dot(left[:, 0:128], own_right, 0, 0))
        low = entries(dot(left[:, 128:256], own_right[:, 128:256], 0, 0))
        kb[q, pl.ds(0, 128), pl.ds(0, LEAF)] = top
        kb[q, pl.ds(128, 128), pl.ds(128, 128)] = low
        kb[q, pl.ds(128, 128), pl.ds(0, 128)] = top[:, 128:256].T
        for b in range(1, HW + 1):
            kb[q, :, pl.ds(b * LEAF, LEAF)] = entries(dot(left, fb[:, cols(q + HW + b)], 0, 0))

    def near_main(i):
        e = i + HW
        mine = vx[:, cols(e)]
        total = None
        parts = []
        for o in range(HW + 1):
            block = kb[i, :, pl.ds(o * LEAF, LEAF)]
            term = dot(vx[:, cols(e + o)], block, 1, 1) * often(i, HW + o)
            total = term if total is None else total + term
            if o:
                parts.append(dot(mine, block, 1, 0) * often(i + o, HW - o))
        acc[:, cols(e, HW + 1)] += jnp.concatenate([total] + parts, axis=1)

    def joined(read, m):
        return jnp.concatenate(
            [jnp.concatenate([read(2 * j), read(2 * j + 1)], axis=1) for j in range(m)], axis=0
        )

    def upward(src, at, dst, to, m, weight):
        high = src.shape[1]
        whole = dot(joined(lambda j: src[at + j], m), wup[weight]).astype(BF16)
        for j in range(m):
            dst[to + j] = whole[high * j : high * j + high]

    def levels(stage, weight):
        buf, size = stage[:2]
        at, m = 0, size
        while m > 2:
            upward(buf, at, buf, at + m, m // 2, weight)
            at, m, weight = at + m, m // 2, weight + 1
        return at, weight

    def merged(stage, weight):
        at, weight = levels(stage, weight)
        return dot(joined(lambda j: stage[0][at + j], 1), wup[weight]).astype(BF16)

    def depth(size):
        return (size - 1).bit_length()

    def enter():
        pl.semaphore_wait(barrier, 3 + c + (zn - 1) + (xn - 1) + (yn - 1))
        for copy in (sb, sv):
            copy.start()

        @pl.when(c == 0)
        def _():
            sp.start()
            st.start()

        sr.start()
        sl.start()
        weights()

    lanes = lax.broadcasted_iota(jnp.int32, (32, 128), 1) < 64

    def coefficients():
        lv.wait()
        sv.wait_recv()
        lb.wait()
        sb.wait_recv()
        lt.wait()

        @pl.loop(0, OWN, step=8)
        def _(i0):
            for k in range(8):
                i = i0 + k
                mine = bx[16 * c + i]
                full = dot(
                    vx[:, cols(i + HW)], jnp.concatenate([mine, mine], axis=0), 1, 1
                )
                dco[i] = full.astype(BF16)
                lev[i] = jnp.where(lanes, full[0:32], full[32:64]).astype(BF16)

        upward(lev, 0, lev, 16, 8, 0)
        upward(lev, 16, lev, 24, 4, 0)
        upward(lev, 24, lev, 28, 2, 0)
        whole = dot(joined(lambda j: lev[28 + j], 1), wup[0]).astype(BF16)
        lev[30] = whole
        pair[c] = whole
        sn.start()
        for copy in (sc, se0, se1, lf):
            copy.start()

    def z_stage():
        sn.wait_recv()
        root = dot(joined(lambda j: pair[j], 1), wroot[...])
        zb[z] = jnp.where(lanes[0:16], root[0:16], root[16:32]).astype(BF16)
        ring_start(stages[0])

    def x_stage():
        ring_recv(stages[0])
        xb[x] = merged(stages[0], 1)
        ring_start(stages[1])

    def y_stage():
        ring_recv(stages[1])
        yb[y] = merged(stages[1], 1 + depth(zn))
        ring_start(stages[2])

    def rims():
        @pl.when(c == 1)
        def _():
            sp.wait_recv()
            for r in range(2):
                arrived(vx.at[pl.ds(0, 32), cols(20, 4)], 4 + r)
            st.wait_recv()
            lu.start()
            for e in range(4):
                factors(e + 20)
            lu.wait()

    def place(k):
        at = SCHEDULE[-1][k]
        for row in range(1, len(SCHEDULE) - 1):
            at = jnp.where(z == row - 1, SCHEDULE[row][k], at)
        return jnp.where(d == 0, SCHEDULE[0][k], at)

    ahead = place(0)
    last = place(5)
    events = tuple(
        (place(k + 1), event)
        for k, event in enumerate((coefficients, z_stage, x_stage, y_stage))
    ) + ((last, rims), (last + HW + 1, ss.start))

    lp.wait()

    @pl.loop(0, 20, step=4)
    def _(e):
        for k in range(4):
            factors(e + k + 4 - 4 * c)

    acc[...] = jnp.zeros_like(acc)
    fco[40] = jnp.zeros((32, 128), BF16)
    counts()

    @pl.loop(0, ahead)
    def _(t):
        kernel_row(2 * t)
        kernel_row(2 * t + 1)

    enter()

    @pl.loop(0, 20 - 2 * ahead)
    def _(t):
        for when, event in events:
            pl.when(t == when)(event)
        left = 17 - 2 * ahead
        here = t - last
        kernels = (here < HW) | ((here > HW) & (t < left))

        @pl.when(kernels)
        def _():
            row = jnp.where(here < HW, here + 12, 2 * ahead + t - HW - 1)
            kernel_row(jnp.where(here < 0, 2 * ahead + t, row))

        @pl.when(jnp.logical_not(kernels))
        def _():
            i = 4 * jnp.where(t < left, 3, t - left)
            for k in range(4):
                near_main(i + k)

    ss.wait_recv()
    acc[:, cols(HW, HW)] += spill[...]
    so.start()
    ln.start()

    lf.wait()
    sc.wait_recv()
    for r in range(2):
        arrived(fco.at[pl.ds(0, HW)], 7 + r)
    lc.wait()
    pick0 = jnp.where(lanes, 1.0, 0.0).astype(BF16)
    pick1 = jnp.where(lanes, 0.0, 1.0).astype(BF16)

    ring_recv(stages[2])

    for i in range(32):
        used = far_count[i]
        at = [jnp.where(s < used, far_list[s, i] - d * 32 + HW, 40) for s in range(8)]
        coeffs = jnp.concatenate(
            [fco[at[2 * q]] * pick0 + fco[at[2 * q + 1]] * pick1 for q in range(4)], axis=1
        )
        yfar[i] = dot(coeffs, cv[i].reshape(512, 64))

    levels(stages[2], 1 + depth(zn) + depth(xn))

    down = jnp.zeros((16, 128), BF16)
    u = upl - 1
    for buf, size, me, _, _, _ in reversed(stages):
        for step in range(depth(size) - 1, -1, -1):
            here = me // 2**step
            side = lax.rem(here, 2)
            sibling = buf[2 * size - 2 * (size >> step) + here + 1 - 2 * side]
            both = jnp.concatenate([sibling, down], axis=1)
            down = dot(both, wdn[2 * u + side]).astype(BF16)
            u -= 1

    nodes[0] = down
    at, m = 0, 1
    while m < OWN:
        whole = jnp.concatenate([nodes[at + j] for j in range(m)], axis=0)
        child = dot(whole, wld[...]).astype(BF16)
        for j in range(m):
            for s in range(2):
                nodes[at + m + 2 * j + s] = child[
                    16 * j : 16 * j + 16, 128 * s : 128 * s + 128
                ]
        at, m = at + m, 2 * m
    whole = jnp.concatenate([nodes[at + j] for j in range(OWN)], axis=0)
    for h in range(2):
        low = dot(whole, wleaf[h])
        for j in range(OWN):
            for s in range(2):
                ldown[2 * j + s, pl.ds(16 * h, 16), :] = low[
                    16 * j : 16 * j + 16, 128 * s : 128 * s + 128
                ]

    sl.wait_recv()
    ln.wait()
    so.wait_recv()

    @pl.loop(0, 32, step=8)
    def _(i0):
        for k in range(8):
            i = i0 + k
            leaf_local = (yfar[i] + ldown[i][:, 0:64]).astype(BF16)
            out[:, cols(i)] += dot(leaf_local, bx[i])

    for copy in (sv, sb, sl, sr, sc, se0, se1, sn, ss, so):
        copy.wait_send()

    @pl.when(c == 0)
    def _():
        sp.wait_send()
        st.wait_send()

    for stage in stages:

        @pl.loop(1, stage[1])
        def _(t):
            ring(stage, t).wait_send()


def solution(mesh):
    n = mesh.shape["leaf"]
    dims = (4, 4, 8) if n == 128 else (2, 2, n // 4)
    yn, xn, zn = dims
    upl = (n - 1).bit_length()
    hbm = pl.BlockSpec(memory_space=pltpu.HBM)
    vmem = pl.BlockSpec(memory_space=pltpu.VMEM)
    smem = pl.BlockSpec(memory_space=pltpu.SMEM)
    dma = pltpu.SemaphoreType.DMA

    def on_device(values, points, basis, near_list, far_list, *rest):
        return pl.pallas_call(
            functools.partial(kernel, dims),
            out_shape=pltpu.VMEM((32, 8192), F32),
            in_specs=[hbm, hbm, hbm, vmem, smem, smem, hbm, vmem, vmem, vmem],
            out_specs=vmem,
            scratch_shapes=[
                pltpu.VMEM((64, EXT * LEAF), BF16),
                pltpu.VMEM((3, EXT * LEAF), F32),
                pltpu.VMEM((32, EXT * LEAF), BF16),
                pltpu.VMEM((32, EXT * LEAF), BF16),
                pltpu.VMEM((32, 64, LEAF), BF16),
                pltpu.VMEM((32, 8, 64, 64), BF16),
                pltpu.VMEM((OWN, LEAF, (HW + 1) * LEAF), BF16),
                pltpu.VMEM((64, EXT * LEAF), F32),
                pltpu.VMEM((OWN, 64, 128), BF16),
                pltpu.VMEM((41, 32, 128), BF16),
                pltpu.VMEM((31, 32, 128), BF16),
                pltpu.VMEM((32, 32, 128), F32),
                pltpu.VMEM((32, 32, 64), F32),
                pltpu.VMEM((31, 16, 128), BF16),
                pltpu.VMEM((2, 32, 128), BF16),
                pltpu.VMEM((2 * zn, 16, 128), BF16),
                pltpu.VMEM((2 * xn, 16, 128), BF16),
                pltpu.VMEM((2 * yn, 16, 128), BF16),
                pltpu.VMEM((upl, 256, 128), BF16),
                pltpu.VMEM((2 * upl, 256, 128), BF16),
                pltpu.VMEM((128, 256), BF16),
                pltpu.VMEM((256, 128), BF16),
                pltpu.VMEM((2, 128, 256), BF16),
                pltpu.VMEM((16, 128), F32),
                pltpu.VMEM((16, 128), F32),
                pltpu.SMEM((16, 128), F32),
                pltpu.SMEM((16, 128), F32),
                pltpu.VMEM((64, HW * LEAF), F32),
                dma((8,)),
                dma((12,)),
                dma((13,)),
                dma((zn - 1,)),
                dma((zn - 1,)),
                dma((xn - 1,)),
                dma((xn - 1,)),
                dma((yn - 1,)),
                dma((yn - 1,)),
            ],
            compiler_params=pltpu.CompilerParams(
                collective_id=0, has_side_effects=True, vmem_limit_bytes=56 * 2**20
            ),
            name="h2_matvec",
        )(values, points, basis, near_list.T, far_list.T, *rest)

    placed = (
        P("rhs", "leaf"),
        P(None, "leaf"),
        P("leaf", "rhs", None),
        P("leaf", None),
        P("leaf", None),
        P("leaf"),
        P("leaf", None, None, None),
        P(),
        P(),
        P(),
    )
    return jax.shard_map(
        on_device, mesh=mesh, in_specs=placed, out_specs=P("rhs", "leaf"), check_vma=False
    )
```

```python
import functools
import math

import jax
import jax.numpy as jnp
import numpy as np
from jax import lax
from jax.experimental import pallas as pl
from jax.experimental.pallas import tpu as pltpu
from jax.sharding import PartitionSpec as P

MESH = pl.DeviceIdType.MESH
F32 = jnp.float32
BF16 = jnp.bfloat16
HW = 4
WAVE = 20.0
SMOOTH = 0.05
LEAF = 256
OWN = 16
EXT = OWN + 2 * HW
SCALE = WAVE / (2 * math.pi)
SOFT = SCALE * SCALE * SMOOTH * SMOOTH
DEGREE = 4
SCHEDULE = (
    (4, 0, 0, 4, 9, 0),
    (3, 0, 0, 4, 9, 1),
    (2, 0, 0, 4, 9, 1),
    (2, 0, 0, 4, 9, 1),
    (1, 0, 0, 4, 9, 1),
    (1, 0, 0, 5, 9, 1),
)


def cosine_fit():
    nodes = 0.125 + 0.125 * np.cos(np.pi * (np.arange(64) + 0.5) / 64)
    series = np.polynomial.chebyshev.Chebyshev.fit(
        nodes, np.cos(2 * np.pi * np.sqrt(nodes)), DEGREE, domain=[0, 0.25]
    )
    return [float(v) for v in series.convert(kind=np.polynomial.Polynomial).coef]


COSINE = cosine_fit()
FACTOR = COSINE[DEGREE] * SCALE / math.sqrt(9 * LEAF)


def entries(scaled):
    scaled = jnp.maximum(scaled, 1e-12)
    turns = scaled * lax.rsqrt(scaled)
    rest = turns - jnp.round(turns)
    square = rest * rest
    poly = square + COSINE[DEGREE - 1] / COSINE[DEGREE]
    for power in range(DEGREE - 2, -1, -1):
        poly = poly * square + COSINE[power] / COSINE[DEGREE]
    return (poly * lax.rsqrt(scaled + SOFT)).astype(BF16)


def dot(a, b, left=1, right=0):
    return lax.dot_general(a, b, (((left,), (right,)), ((), ())), preferred_element_type=F32)


def cols(leaf, count=1):
    return pl.ds(pl.multiple_of(leaf * LEAF, LEAF), count * LEAF)


def diagonal(block):
    block = block.astype(F32)
    zero = jnp.zeros_like(block)
    top = jnp.concatenate([block, zero], axis=1)
    low = jnp.concatenate([zero, block], axis=1)
    return jnp.concatenate([top, low], axis=0).astype(BF16)


def kernel(
    dims,
    values,
    points,
    basis,
    near_list,
    far_list,
    far_count,
    couple,
    local_transfer,
    upper_transfer,
    upper_couple,
    out,
    vx,
    px,
    fa,
    fb,
    bx,
    cv,
    kb,
    acc,
    dco,
    fco,
    lev,
    ldown,
    yfar,
    nodes,
    pair,
    zb,
    xb,
    yb,
    wup,
    wdn,
    wld,
    wroot,
    wleaf,
    tally,
    tally_next,
    count,
    count_next,
    spill,
    loc,
    ssem,
    rsem,
    zs,
    zr,
    xs,
    xr,
    ys,
    yr,
):
    yn, xn, zn = dims
    n = yn * xn * zn
    d = lax.axis_index("leaf")
    c = lax.axis_index("rhs")
    p = 1 - c
    z = lax.rem(d, zn)
    x = lax.rem(d // zn, xn)
    y = d // (zn * xn)
    after = lax.rem(d + 1, n)
    before = lax.rem(d + n - 1, n)
    beside = lax.rem(d + n - 1 + 2 * c, n)
    upl = (n - 1).bit_length()
    own = pl.ds(32 * c, 32)

    barrier = pltpu.get_barrier_semaphore()

    def greet(leaf, core):
        pl.semaphore_signal(barrier, inc=1, device_id=(leaf, core), device_id_type=MESH)

    def z_peer(t):
        return d - z + lax.rem(z + t, zn)

    def x_peer(t):
        return d + (lax.rem(x + t, xn) - x) * zn

    def y_peer(t):
        return d + (lax.rem(y + t, yn) - y) * zn * xn

    stages = (
        (zb, zn, z, zs, zr, z_peer),
        (xb, xn, x, xs, xr, x_peer),
        (yb, yn, y, ys, yr, y_peer),
    )

    greet(d, p)
    greet(before, 1)
    greet(after, 0)

    @pl.when(c == 1)
    def _():
        greet(after, 1)

    for _, size, _, _, _, peer in stages:

        @pl.loop(1, size)
        def _(t):
            greet(peer(t), c)

    def local(src, dst, k):
        return pltpu.make_async_copy(src, dst, loc.at[k])

    lp = local(points.at[:, cols(12 * c, 20)], px.at[:, cols(4 - 4 * c, 20)], 0)
    lv = local(
        values.at[:, cols(12 * c, 20)], vx.at[own, cols(4 - 4 * c, 20)], 1
    )
    lb = local(basis, bx.at[:, own, :], 2)
    lc = local(couple, cv, 3)
    lf = local(dco.at[:, own, :], fco.at[pl.ds(16 * c + HW, OWN)], 4)
    lt = local(tally, count, 6)
    lu = local(tally_next, count_next, 7)
    ln = local(acc.at[own, cols(HW, OWN)], out.at[:, cols(16 * c, OWN)], 5)
    for copy in (lp, lv, lb, lc):
        copy.start()

    def remote(src, dst, k, r, leaf, core):
        return pltpu.make_async_remote_copy(
            src_ref=src,
            dst_ref=dst,
            send_sem=ssem.at[k],
            recv_sem=rsem.at[r],
            device_id=(leaf, core),
            device_id_type=MESH,
        )

    sv = remote(values.at[:, cols(12 * p, 20)], vx.at[own, cols(4 - 4 * p, 20)], 0, 0, d, p)
    sb = remote(
        basis.at[pl.ds(16 * p, 16)], bx.at[pl.ds(16 * p, 16), own, :], 1, 1, d, p
    )
    sl = remote(
        basis.at[pl.ds(16 * c, 16)], bx.at[pl.ds(16 * c, 16), own, :], 2, 2, d, p
    )
    sp = remote(points.at[:, cols(0, 4)], px.at[:, cols(20, 4)], 3, 3, before, 1)
    st = remote(tally, tally_next, 4, 11, before, 1)
    sr = remote(values.at[:, cols(0, 4)], vx.at[own, cols(20, 4)], 5, 4 + c, before, 1)
    ss = remote(
        acc.at[:, cols(20, 4)], spill, 11, 12, lax.rem(d + c, n), p
    )
    sc = remote(
        dco.at[:, pl.ds(32 * p, 32), :], fco.at[pl.ds(16 * c + HW, OWN)], 6, 6, d, p
    )
    se0, se1 = [
        remote(
            dco.at[pl.ds(12 * c, HW), pl.ds(32 * q, 32), :],
            fco.at[pl.ds(36 * p, HW)],
            7 + q,
            7 + c,
            beside,
            q,
        )
        for q in range(2)
    ]
    sn = remote(lev.at[30], pair.at[c], 9, 9, d, p)
    so = remote(
        acc.at[pl.ds(32 * p, 32), cols(HW, OWN)], out.at[:, cols(16 * c, OWN)], 10, 10, d, p
    )

    def arrived(ref, r):
        pltpu.make_async_copy(ref, ref, rsem.at[r]).wait()

    def ring(stage, t):
        buf, size, me, sems, recvs, peer = stage
        return pltpu.make_async_remote_copy(
            src_ref=buf.at[me],
            dst_ref=buf.at[me],
            send_sem=sems.at[t - 1],
            recv_sem=recvs.at[t - 1],
            device_id=(peer(t), c),
            device_id_type=MESH,
        )

    def ring_start(stage):
        @pl.loop(1, stage[1])
        def _(t):
            ring(stage, t).start()

    def ring_recv(stage):
        @pl.loop(1, stage[1])
        def _(t):
            ring(stage, t).wait_recv()

    def weights():
        zero = jnp.zeros((64, 64), F32)
        none = jnp.zeros((64, 128), BF16)
        for s in range(2):
            t = local_transfer[s]
            wup[0, pl.ds(128 * s, 128), :] = diagonal(t)
            td = t.astype(F32).T
            wld[:, pl.ds(128 * s, 128)] = diagonal(td)
            tf = t.astype(F32)
            wroot[pl.ds(128 * s + 64 * c, 64), :] = jnp.concatenate(
                [tf, tf], axis=1
            ).astype(BF16)
            wroot[pl.ds(128 * s + 64 * p, 64), :] = none
            wide = jnp.concatenate([td, zero], axis=1).astype(BF16)
            wleaf[0, pl.ds(0, 64), pl.ds(128 * s, 128)] = wide
            wleaf[0, pl.ds(64, 64), pl.ds(128 * s, 128)] = none
            wleaf[1, pl.ds(0, 64), pl.ds(128 * s, 128)] = none
            wleaf[1, pl.ds(64, 64), pl.ds(128 * s, 128)] = wide
        for u in range(upl):
            for s in range(2):
                t = upper_transfer[u, s]
                if u < upl - 1:
                    wup[u + 1, pl.ds(128 * s, 128), :] = diagonal(t)
                wdn[2 * u + s, pl.ds(0, 128), :] = diagonal(upper_couple[u, s])
                wdn[2 * u + s, pl.ds(128, 128), :] = diagonal(t.astype(F32).T)

    def counts():
        leaf = lax.broadcasted_iota(jnp.int32, (9, 32), 1)
        offset = near_list[...] - leaf - d * 32
        tally[...] = jnp.zeros_like(tally)
        for o in range(9):
            same = jnp.where(offset == o - HW, FACTOR, 0.0)
            tally[pl.ds(o, 1), pl.ds(0, 32)] = jnp.sum(same, axis=0, keepdims=True)
        lt.start()

    def often(i, o):
        row = 16 * c + i
        return jnp.where(
            row < 32, count[o, row], count_next[o, jnp.maximum(row - 32, 0)]
        )

    rows = lax.broadcasted_iota(jnp.int32, (8, LEAF), 0)

    def factors(e):
        at = cols(e)
        pts = (px[:, at] - 0.5) * SCALE
        pts = jnp.concatenate([pts, jnp.zeros((5, LEAF), F32)], axis=0)
        high = pts.astype(BF16).astype(F32)
        low = (pts - high).astype(BF16).astype(F32)
        both = high + low
        norm = jnp.sum(both * both, axis=0, keepdims=True)
        n1 = norm.astype(BF16).astype(F32)
        n2 = (norm - n1).astype(BF16).astype(F32)
        n3 = (norm - n1 - n2).astype(BF16).astype(F32)
        norms = jnp.where(
            rows == 3, n1, jnp.where(rows == 4, n2, jnp.where(rows == 5, n3, 0.0))
        )
        ones = jnp.where((rows >= 3) & (rows <= 5), 1.0, 0.0)
        fa[:, at] = jnp.concatenate([high + norms, high + ones, low, low], axis=0).astype(BF16)
        fb[:, at] = jnp.concatenate(
            [ones - 2 * high, norms - 2 * low, -2 * high, -2 * low], axis=0
        ).astype(BF16)

    def kernel_row(q):
        left = fa[:, cols(q + HW)]
        own_right = fb[:, cols(q + HW)]
        top = entries(dot(left[:, 0:128], own_right, 0, 0))
        low = entries(dot(left[:, 128:256], own_right[:, 128:256], 0, 0))
        kb[q, pl.ds(0, 128), pl.ds(0, LEAF)] = top
        kb[q, pl.ds(128, 128), pl.ds(128, 128)] = low
        kb[q, pl.ds(128, 128), pl.ds(0, 128)] = top[:, 128:256].T
        for b in range(1, HW + 1):
            kb[q, :, pl.ds(b * LEAF, LEAF)] = entries(dot(left, fb[:, cols(q + HW + b)], 0, 0))

    def near_main(i):
        e = i + HW
        mine = vx[:, cols(e)]
        total = None
        parts = []
        for o in range(HW + 1):
            block = kb[i, :, pl.ds(o * LEAF, LEAF)]
            term = dot(vx[:, cols(e + o)], block, 1, 1) * often(i, HW + o)
            total = term if total is None else total + term
            if o:
                parts.append(dot(mine, block, 1, 0) * often(i + o, HW - o))
        acc[:, cols(e, HW + 1)] += jnp.concatenate([total] + parts, axis=1)

    def joined(read, m):
        return jnp.concatenate(
            [jnp.concatenate([read(2 * j), read(2 * j + 1)], axis=1) for j in range(m)], axis=0
        )

    def upward(src, at, dst, to, m, weight):
        high = src.shape[1]
        whole = dot(joined(lambda j: src[at + j], m), wup[weight]).astype(BF16)
        for j in range(m):
            dst[to + j] = whole[high * j : high * j + high]

    def levels(stage, weight):
        buf, size = stage[:2]
        at, m = 0, size
        while m > 2:
            upward(buf, at, buf, at + m, m // 2, weight)
            at, m, weight = at + m, m // 2, weight + 1
        return at, weight

    def merged(stage, weight):
        at, weight = levels(stage, weight)
        return dot(joined(lambda j: stage[0][at + j], 1), wup[weight]).astype(BF16)

    def depth(size):
        return (size - 1).bit_length()

    def enter():
        pl.semaphore_wait(barrier, 3 + c + (zn - 1) + (xn - 1) + (yn - 1))
        for copy in (sb, sv):
            copy.start()

        @pl.when(c == 0)
        def _():
            sp.start()
            st.start()

        sr.start()
        sl.start()
        weights()

    lanes = lax.broadcasted_iota(jnp.int32, (32, 128), 1) < 64

    def coefficients():
        lv.wait()
        sv.wait_recv()
        lb.wait()
        sb.wait_recv()
        lt.wait()

        for i0 in range(0, OWN, 8):
            for k in range(8):
                i = i0 + k
                mine = bx[16 * c + i]
                full = dot(
                    vx[:, cols(i + HW)], jnp.concatenate([mine, mine], axis=0), 1, 1
                )
                dco[i] = full.astype(BF16)
                lev[i] = jnp.where(lanes, full[0:32], full[32:64]).astype(BF16)

        upward(lev, 0, lev, 16, 8, 0)
        upward(lev, 16, lev, 24, 4, 0)
        upward(lev, 24, lev, 28, 2, 0)
        whole = dot(joined(lambda j: lev[28 + j], 1), wup[0]).astype(BF16)
        lev[30] = whole
        pair[c] = whole
        sn.start()
        for copy in (sc, se0, se1, lf):
            copy.start()

    def z_stage():
        sn.wait_recv()
        root = dot(joined(lambda j: pair[j], 1), wroot[...])
        zb[z] = jnp.where(lanes[0:16], root[0:16], root[16:32]).astype(BF16)
        ring_start(stages[0])

    def x_stage():
        ring_recv(stages[0])
        xb[x] = merged(stages[0], 1)
        ring_start(stages[1])

    def y_stage():
        ring_recv(stages[1])
        yb[y] = merged(stages[1], 1 + depth(zn))
        ring_start(stages[2])

    def rims():
        @pl.when(c == 1)
        def _():
            sp.wait_recv()
            for r in range(2):
                arrived(vx.at[pl.ds(0, 32), cols(20, 4)], 4 + r)
            st.wait_recv()
            lu.start()
            for e in range(4):
                factors(e + 20)
            lu.wait()

    def place(k):
        at = SCHEDULE[-1][k]
        for row in range(1, len(SCHEDULE) - 1):
            at = jnp.where(z == row - 1, SCHEDULE[row][k], at)
        return jnp.where(d == 0, SCHEDULE[0][k], at)

    sends = (d < n - 1) | (c == 0)
    takes = (d > 0) | (c == 1)

    def spill_start():
        pl.when(sends)(ss.start)

    ahead = place(0)
    last = place(5)
    events = tuple(
        (place(k + 1), event)
        for k, event in enumerate((coefficients, z_stage, x_stage, y_stage))
    ) + ((last, rims), (last + HW + 1, spill_start))

    lp.wait()

    @pl.loop(0, 20, step=4)
    def _(e):
        for k in range(4):
            factors(e + k + 4 - 4 * c)

    acc[...] = jnp.zeros_like(acc)
    fco[40] = jnp.zeros((32, 128), BF16)
    counts()

    @pl.loop(0, ahead)
    def _(t):
        kernel_row(2 * t)
        kernel_row(2 * t + 1)

    enter()

    @pl.loop(0, 20 - 2 * ahead)
    def _(t):
        for when, event in events:
            pl.when(t == when)(event)
        left = 17 - 2 * ahead
        here = t - last
        kernels = (here < HW) | ((here > HW) & (t < left))

        @pl.when(kernels)
        def _():
            row = jnp.where(here < HW, here + 12, 2 * ahead + t - HW - 1)
            kernel_row(jnp.where(here < 0, 2 * ahead + t, row))

        @pl.when(jnp.logical_not(kernels))
        def _():
            i = 4 * jnp.where(t < left, 3, t - left)
            for k in range(4):
                near_main(i + k)

    @pl.when(takes)
    def _():
        ss.wait_recv()
        acc[:, cols(HW, HW)] += spill[...]

    so.start()
    ln.start()

    lf.wait()
    sc.wait_recv()
    for r in range(2):
        arrived(fco.at[pl.ds(0, HW)], 7 + r)
    lc.wait()
    pick0 = jnp.where(lanes, 1.0, 0.0).astype(BF16)
    pick1 = jnp.where(lanes, 0.0, 1.0).astype(BF16)

    ring_recv(stages[2])

    for i in range(32):
        used = far_count[i]
        at = [jnp.where(s < used, far_list[s, i] - d * 32 + HW, 40) for s in range(8)]
        coeffs = jnp.concatenate(
            [fco[at[2 * q]] * pick0 + fco[at[2 * q + 1]] * pick1 for q in range(4)], axis=1
        )
        yfar[i] = dot(coeffs, cv[i].reshape(512, 64))

    levels(stages[2], 1 + depth(zn) + depth(xn))

    down = jnp.zeros((16, 128), BF16)
    u = upl - 1
    for buf, size, me, _, _, _ in reversed(stages):
        for step in range(depth(size) - 1, -1, -1):
            here = me // 2**step
            side = lax.rem(here, 2)
            sibling = buf[2 * size - 2 * (size >> step) + here + 1 - 2 * side]
            both = jnp.concatenate([sibling, down], axis=1)
            down = dot(both, wdn[2 * u + side]).astype(BF16)
            u -= 1

    nodes[0] = down
    at, m = 0, 1
    while m < OWN:
        whole = jnp.concatenate([nodes[at + j] for j in range(m)], axis=0)
        child = dot(whole, wld[...]).astype(BF16)
        for j in range(m):
            for s in range(2):
                nodes[at + m + 2 * j + s] = child[
                    16 * j : 16 * j + 16, 128 * s : 128 * s + 128
                ]
        at, m = at + m, 2 * m
    whole = jnp.concatenate([nodes[at + j] for j in range(OWN)], axis=0)
    for h in range(2):
        low = dot(whole, wleaf[h])
        for j in range(OWN):
            for s in range(2):
                ldown[2 * j + s, pl.ds(16 * h, 16), :] = low[
                    16 * j : 16 * j + 16, 128 * s : 128 * s + 128
                ]

    sl.wait_recv()
    ln.wait()
    so.wait_recv()

    @pl.loop(0, 32, step=8)
    def _(i0):
        for k in range(8):
            i = i0 + k
            leaf_local = (yfar[i] + ldown[i][:, 0:64]).astype(BF16)
            out[:, cols(i)] += dot(leaf_local, bx[i])

    for copy in (sv, sb, sl, sr, sc, se0, se1, sn, so):
        copy.wait_send()
    pl.when(sends)(ss.wait_send)

    @pl.when(c == 0)
    def _():
        sp.wait_send()
        st.wait_send()

    for stage in stages:

        @pl.loop(1, stage[1])
        def _(t):
            ring(stage, t).wait_send()


def solution(mesh):
    n = mesh.shape["leaf"]
    dims = (4, 4, 8) if n == 128 else (2, 2, n // 4)
    yn, xn, zn = dims
    upl = (n - 1).bit_length()
    hbm = pl.BlockSpec(memory_space=pltpu.HBM)
    vmem = pl.BlockSpec(memory_space=pltpu.VMEM)
    smem = pl.BlockSpec(memory_space=pltpu.SMEM)
    dma = pltpu.SemaphoreType.DMA

    def on_device(values, points, basis, near_list, far_list, *rest):
        return pl.pallas_call(
            functools.partial(kernel, dims),
            out_shape=pltpu.VMEM((32, 8192), F32),
            in_specs=[hbm, hbm, hbm, vmem, smem, smem, hbm, vmem, vmem, vmem],
            out_specs=vmem,
            scratch_shapes=[
                pltpu.VMEM((64, EXT * LEAF), BF16),
                pltpu.VMEM((3, EXT * LEAF), F32),
                pltpu.VMEM((32, EXT * LEAF), BF16),
                pltpu.VMEM((32, EXT * LEAF), BF16),
                pltpu.VMEM((32, 64, LEAF), BF16),
                pltpu.VMEM((32, 8, 64, 64), BF16),
                pltpu.VMEM((OWN, LEAF, (HW + 1) * LEAF), BF16),
                pltpu.VMEM((64, EXT * LEAF), F32),
                pltpu.VMEM((OWN, 64, 128), BF16),
                pltpu.VMEM((41, 32, 128), BF16),
                pltpu.VMEM((31, 32, 128), BF16),
                pltpu.VMEM((32, 32, 128), F32),
                pltpu.VMEM((32, 32, 64), F32),
                pltpu.VMEM((31, 16, 128), BF16),
                pltpu.VMEM((2, 32, 128), BF16),
                pltpu.VMEM((2 * zn, 16, 128), BF16),
                pltpu.VMEM((2 * xn, 16, 128), BF16),
                pltpu.VMEM((2 * yn, 16, 128), BF16),
                pltpu.VMEM((upl, 256, 128), BF16),
                pltpu.VMEM((2 * upl, 256, 128), BF16),
                pltpu.VMEM((128, 256), BF16),
                pltpu.VMEM((256, 128), BF16),
                pltpu.VMEM((2, 128, 256), BF16),
                pltpu.VMEM((16, 128), F32),
                pltpu.VMEM((16, 128), F32),
                pltpu.SMEM((16, 128), F32),
                pltpu.SMEM((16, 128), F32),
                pltpu.VMEM((64, HW * LEAF), F32),
                dma((8,)),
                dma((12,)),
                dma((13,)),
                dma((zn - 1,)),
                dma((zn - 1,)),
                dma((xn - 1,)),
                dma((xn - 1,)),
                dma((yn - 1,)),
                dma((yn - 1,)),
            ],
            compiler_params=pltpu.CompilerParams(
                collective_id=0, has_side_effects=True, vmem_limit_bytes=56 * 2**20
            ),
            name="h2_matvec",
        )(values, points, basis, near_list.T, far_list.T, *rest)

    placed = (
        P("rhs", "leaf"),
        P(None, "leaf"),
        P("leaf", "rhs", None),
        P("leaf", None),
        P("leaf", None),
        P("leaf"),
        P("leaf", None, None, None),
        P(),
        P(),
        P(),
    )
    return jax.shard_map(
        on_device, mesh=mesh, in_specs=placed, out_specs=P("rhs", "leaf"), check_vma=False
    )
```
